512 devices in a mesh: ctx: 32 (over z_hi, y, x), chan: 16 (over z_lo, core).
Axes of the slice: x: 4, y: 4, z: 16 (z_hi: 2, z_lo: 8; z = z_hi * 8 + z_lo), core: 2. Of those that a mesh axis runs over, the one named last changes fastest.
Arguments:
- key_branch: float32 [4096, 4096], P('ctx', 'chan'), may hold values from -6 to 6
- value_branch: float32 [4096, 4096], P('ctx', 'chan'), may hold values from -6 to 6
- query_branch: float32 [4096, 4096], P('ctx', 'chan'), may hold values from -6 to 6
- long_filter: float32 [4096, 4096], P('ctx', 'chan'), may hold values from -6 to 6
- skip_weight: float32 [4096], P('chan'), may hold values from -4 to 4
- out_weight: float32 [4096, 4096], P('chan', 'ctx'), may hold values from -0.09375 to 0.09375
- cotangent: float32 [4096, 4096], P('ctx', 'chan'), may hold values from -6 to 6
Outputs:
- projected: float32 [4096, 4096], P('ctx', 'chan')
- key_grad: float32 [4096, 4096], P('ctx', 'chan')
- value_grad: float32 [4096, 4096], P('ctx', 'chan')
- query_grad: float32 [4096, 4096], P('ctx', 'chan')
- filter_grad: float32 [4096, 4096], P('ctx', 'chan')
- skip_grad: float32 [4096], P('chan')
- weight_grad: float32 [4096, 4096], P('chan', 'ctx')
The draws below stay inside these ranges and needn't reach their ends.
All inputs are finite; a program needn't handle non-finite values.
Results may differ from the reference program's by a relative error of at most 0.000076.
Values sent between devices are 32-bit elements; how exact they have to be, the bound alone decides.
No kernel may reach another device: no remote copies, remote signals or barrier semaphores. Data moves between devices by JAX's collectives and lax.ppermute only.
A program may use at most 64 MiB of HBM per device.

```python
import jax
import jax.numpy as jnp
from jax import lax

D = 4096
SEQ = 4096


def level_of(key, shape, cuts, low, top_value):
    level = 1.0
    for axis_at, parts in cuts:
        draws = jax.random.uniform(jax.random.fold_in(jax.random.fold_in(key, 6), axis_at), (parts,), jnp.float32, low / len(cuts), top_value / len(cuts))
        level = level * jnp.repeat(jnp.exp(draws), shape[axis_at] // parts).reshape((-1,) + (1,) * (len(shape) - 1 - axis_at))
    return level


def scatter_about(rng, shape, spread, reach, split=(), kind=jnp.bfloat16):
    result = jax.random.normal(rng, shape, jnp.float32) * spread
    if len(split) > 0:
        result = level_of(rng, shape, split, -0.22, 0.18) * result
    return jnp.clip(result, min=-reach, max=reach).astype(kind)


def setup_inputs(seed: int = 0) -> dict:
    key_list = jax.random.split(jax.random.key(seed), 8)
    return {
        "key_branch": scatter_about(key_list[0], (SEQ, D), 1.0, 6.0, ((0, 32), (1, 16)), jnp.float32),
        "value_branch": scatter_about(key_list[1], (SEQ, D), 1.0, 6.0, ((0, 32), (1, 16)), jnp.float32),
        "query_branch": scatter_about(key_list[2], (SEQ, D), 1.0, 6.0, ((0, 32), (1, 16)), jnp.float32),
        "long_filter": scatter_about(key_list[3], (SEQ, D), 1.0, 6.0, ((0, 32), (1, 16)), jnp.float32),
        "skip_weight": scatter_about(key_list[4], (D,), 1.0, 4.0, ((0, 16),), jnp.float32),
        "out_weight": scatter_about(key_list[5], (D, D), D ** -0.5, 0.09375, ((0, 16), (1, 32)), jnp.float32),
        "cotangent": scatter_about(key_list[6], (SEQ, D), 1.0, 6.0, ((0, 32), (1, 16)), jnp.float32),
    }


def causal_conv(kernel, signal):
    length = signal.shape[0]
    spectrum = jnp.fft.rfft(kernel, n=2 * length, axis=0) * jnp.fft.rfft(signal, n=2 * length, axis=0)
    return jnp.fft.irfft(spectrum, n=2 * length, axis=0)[:length]


def lagged_sum(leading, trailing):
    length = leading.shape[0]
    spectrum = jnp.fft.rfft(leading, n=2 * length, axis=0) * jnp.conj(jnp.fft.rfft(trailing, n=2 * length, axis=0))
    return jnp.fft.irfft(spectrum, n=2 * length, axis=0)[:length]


def reference(key_branch, value_branch, query_branch, long_filter, skip_weight, out_weight, cotangent):
    norm_scale = 1.0 / (SEQ ** 0.5)
    product = key_branch * value_branch
    filter_taps = long_filter * norm_scale
    convolved = causal_conv(filter_taps, product)
    pre_gate = convolved + skip_weight * product
    mixed_rows = query_branch * pre_gate
    projected = jnp.dot(mixed_rows, out_weight, precision=lax.Precision.HIGHEST, preferred_element_type=jnp.float32)
    mixed_grad = jnp.dot(cotangent, out_weight.T, precision=lax.Precision.HIGHEST, preferred_element_type=jnp.float32)
    query_grad = mixed_grad * pre_gate
    pre_grad = mixed_grad * query_branch
    skip_grad = jnp.sum(pre_grad * product, axis=0) * norm_scale
    product_grad = lagged_sum(pre_grad, filter_taps) + skip_weight * pre_grad
    key_grad = product_grad * value_branch
    value_grad = product_grad * key_branch
    filter_grad = lagged_sum(pre_grad, product) * norm_scale
    weight_grad = jnp.dot(mixed_rows.T, cotangent, precision=lax.Precision.HIGHEST, preferred_element_type=jnp.float32) * norm_scale
    return (projected, key_grad, value_grad, query_grad, filter_grad, skip_grad, weight_grad)
```

```python
import math

import jax
import jax.numpy as jnp
import numpy as np
from jax import lax
from jax.sharding import Mesh
from jax.sharding import PartitionSpec as P

AXES = ("h", "y", "x", "m", "l", "k")
SIZES = (2, 4, 4, 2, 4, 2)
CTX = ("h", "y", "x")
PLANE = ("y", "x")
LINE = ("m", "l")
side = 128
exact = lax.Precision.HIGHEST
close = lax.Precision.HIGH


def tables(seq_len):
    full = 2 * seq_len
    blocks = full // side
    kept = blocks // 2 + 1
    rows = np.arange(kept)
    first = 2.0 * np.pi * np.outer(rows, np.arange(seq_len // side)) / blocks
    turn = 2.0 * np.pi * np.outer(rows, np.arange(side)) / full
    inner = 2.0 * np.pi * np.outer(np.arange(side), np.arange(side)) / side
    weight = np.where((rows == 0) | (rows == blocks // 2), 1.0, 2.0)[:, None] / full
    cos, sin = np.cos(inner), np.sin(inner)
    as32 = lambda a: jnp.asarray(a.astype(np.float32))
    return dict(
        first=as32(np.concatenate([np.cos(first), -np.sin(first)], 0)),
        turn_cos=as32(np.cos(turn))[:, None, :],
        turn_sin=as32(np.sin(turn))[:, None, :],
        inner=as32(np.block([[cos, -sin], [sin, cos]])),
        outer=as32(np.block([[cos, sin], [-sin, cos]])),
        last=as32(np.concatenate([weight * np.cos(first), -weight * np.sin(first)], 0).T),
        kept=kept,
    )


def forward_fourier(signal, tab):
    both = jnp.einsum("kn,ncm->kcm", tab["first"], signal, precision=exact)
    real, imag = both[: tab["kept"]], both[tab["kept"] :]
    turned = jnp.concatenate(
        [real * tab["turn_cos"] + imag * tab["turn_sin"], imag * tab["turn_cos"] - real * tab["turn_sin"]], 2
    )
    return jnp.einsum("kcm,mj->kcj", turned, tab["inner"], precision=exact)


def inverse_fourier(real, imag, tab):
    back = jnp.einsum("kcm,mj->kcj", jnp.concatenate([real, imag], 2), tab["outer"], precision=exact)
    real, imag = back[..., :side], back[..., side:]
    turned = jnp.concatenate(
        [real * tab["turn_cos"] - imag * tab["turn_sin"], imag * tab["turn_cos"] + real * tab["turn_sin"]], 0
    )
    return jnp.einsum("nk,kcm->ncm", tab["last"], turned, precision=exact)


def halves(spectrum):
    return spectrum[..., :side], spectrum[..., side:]


def swap_hm(block):
    pairs = [(h * 2 + m, m * 2 + h) for h in range(2) for m in range(2)]
    return lax.ppermute(block, ("h", "m"), pairs)


def other_h(block):
    return lax.ppermute(block, "h", [(0, 1), (1, 0)])


def local(key_branch, value_branch, query_branch, long_filter, skip_weight, out_weight, cotangent):
    rows, chans = key_branch.shape
    n_ctx = 32
    group = chans // n_ctx
    seq_len = rows * n_ctx
    norm_scale = 1.0 / math.sqrt(seq_len)
    tab = tables(seq_len)
    at_h = lax.axis_index("h")
    at_ctx = lax.axis_index(CTX)

    cot_mine = swap_hm(cotangent)
    cot_line = lax.all_gather(cot_mine, LINE, axis=0)

    product = key_branch * value_branch
    sent = jnp.concatenate(
        [product.T.reshape(n_ctx, group, rows), (long_filter * norm_scale).T.reshape(n_ctx, group, rows)], 1
    )
    signals = lax.all_to_all(sent, CTX, 0, 0)
    query_own = query_branch.T
    query_far = other_h(query_own)
    query_both = jnp.where(at_h == 0, jnp.stack([query_own, query_far]), jnp.stack([query_far, query_own]))

    weights = lax.all_to_all(jnp.broadcast_to(out_weight[None], (16,) + out_weight.shape), PLANE, 0, 0)
    weights = weights.transpose(1, 0, 2).reshape(chans, -1)

    spectra = forward_fourier(signals, tab)
    prod_real, prod_imag = halves(spectra[:, :group])
    taps_real, taps_imag = halves(spectra[:, group:])
    conv = inverse_fourier(
        prod_real * taps_real - prod_imag * taps_imag, prod_real * taps_imag + prod_imag * taps_real, tab
    )
    skip = lax.dynamic_slice(skip_weight, (at_ctx * group,), (group,))[None, :, None]
    chan_product = signals[:, :group]
    gate_chan = conv + skip * chan_product
    gate_pair = gate_chan.reshape(2, 16, group, rows).transpose(1, 0, 2, 3)
    gate_sent = jnp.broadcast_to(gate_pair[None], (2,) + gate_pair.shape).reshape(n_ctx, 2, group, rows)
    gate_got = lax.all_to_all(gate_sent, CTX, 0, 0)
    gate_both = gate_got.transpose(1, 0, 2, 3).reshape(2, chans, rows)
    mixed = query_both * gate_both
    mixed_flat = mixed.transpose(1, 0, 2).reshape(chans, 2 * rows)

    cot_cores = lax.all_to_all(jnp.broadcast_to(cot_line[None], (2,) + cot_line.shape), "k", 0, 0)
    cot_full = (
        cot_cores.reshape(2, 2, 4, rows, chans).transpose(1, 3, 2, 0, 4).reshape(2 * rows, 8 * chans)
    )

    mixed_grad = lax.dot_general(
        weights, cot_full, (((1,), (1,)), ((), ())), precision=close, preferred_element_type=jnp.float32
    )
    mixed_grad = mixed_grad.reshape(chans, 2, rows).transpose(1, 0, 2)
    grad_sent = (mixed_grad * query_both).reshape(2, n_ctx, group, rows).transpose(1, 0, 2, 3)
    grad_got = lax.all_to_all(grad_sent, CTX, 0, 0)
    grad_chan = grad_got.reshape(2, 16, 2, group, rows).sum(0).transpose(1, 0, 2, 3).reshape(n_ctx, group, rows)

    own_grad = lax.dynamic_index_in_dim(mixed_grad, at_h, 0, False)
    far_grad = lax.dynamic_index_in_dim(mixed_grad, 1 - at_h, 0, False)
    own_gate = lax.dynamic_index_in_dim(gate_both, at_h, 0, False)
    query_grad = ((own_grad + other_h(far_grad)) * own_gate).T

    partial = lax.dot_general(
        mixed_flat, weights, (((0,), (0,)), ((), ())), precision=close, preferred_element_type=jnp.float32
    )
    partial = partial.reshape(2, rows, 4, 2, chans).transpose(3, 0, 2, 1, 4).reshape(2, 8, rows, chans)
    partial = lax.all_to_all(partial, "k", 0, 0).sum(0)
    projected = lax.psum_scatter(partial, LINE, scatter_dimension=0, tiled=False)
    projected = swap_hm(projected)

    weight_part = lax.dot_general(
        mixed_flat, cot_full, (((1,), (0,)), ((), ())), precision=close, preferred_element_type=jnp.float32
    )
    weight_part = weight_part.reshape(chans, 16, rows).transpose(1, 0, 2)
    weight_grad = lax.all_to_all(weight_part, PLANE, 0, 0).sum(0) * norm_scale

    grad_real, grad_imag = halves(forward_fourier(grad_chan, tab))
    lead_real = jnp.concatenate([taps_real, prod_real], 1)
    lead_imag = jnp.concatenate([taps_imag, prod_imag], 1)
    grad_real = jnp.concatenate([grad_real, grad_real], 1)
    grad_imag = jnp.concatenate([grad_imag, grad_imag], 1)
    lagged = inverse_fourier(
        grad_real * lead_real + grad_imag * lead_imag, grad_imag * lead_real - grad_real * lead_imag, tab
    )
    prod_grad = lagged[:, :group] + skip * grad_chan
    skip_part = jnp.sum(grad_chan * chan_product, axis=(0, 2)) * norm_scale
    skip_row = jnp.broadcast_to(jnp.pad(skip_part, (0, rows - group))[None, None], (n_ctx, 1, rows))
    back = lax.all_to_all(jnp.concatenate([prod_grad, lagged[:, group:] * norm_scale, skip_row], 1), CTX, 0, 0)
    product_grad = back[:, :group].reshape(chans, rows).T
    filter_grad = back[:, group : 2 * group].reshape(chans, rows).T
    skip_grad = back[:, 2 * group, :group].reshape(chans)
    return (
        projected,
        product_grad * value_branch,
        product_grad * key_branch,
        query_grad,
        filter_grad,
        skip_grad,
        weight_grad,
    )


def solution(mesh):
    grid = Mesh(mesh.devices.reshape(SIZES), AXES)
    wide = P(("h", "y", "x"), ("m", "l", "k"))
    tall = P(("m", "l", "k"), ("h", "y", "x"))
    flat = P(("m", "l", "k"))
    return jax.shard_map(
        local,
        mesh=grid,
        in_specs=(wide, wide, wide, wide, flat, tall, wide),
        out_specs=(wide, wide, wide, wide, wide, flat, tall),
        check_vma=False,
    )
```

```python
import math

import jax
import jax.numpy as jnp
import numpy as np
from jax import lax
from jax.sharding import Mesh
from jax.sharding import PartitionSpec as P

AXES = ("h", "y", "x", "m", "l", "k")
SIZES = (2, 4, 4, 2, 4, 2)
CTX = ("h", "y", "x")
PLANE = ("y", "x")
LINE = ("m", "l")
side = 128
exact = lax.Precision.HIGHEST
close = lax.Precision.HIGH


def tables(seq_len):
    full = 2 * seq_len
    blocks = full // side
    kept = blocks // 2 + 1
    rows = np.arange(kept)
    first = 2.0 * np.pi * np.outer(rows, np.arange(seq_len // side)) / blocks
    turn = 2.0 * np.pi * np.outer(rows, np.arange(side)) / full
    inner = 2.0 * np.pi * np.outer(np.arange(side), np.arange(side)) / side
    weight = np.where((rows == 0) | (rows == blocks // 2), 1.0, 2.0)[:, None] / full
    cos, sin = np.cos(inner), np.sin(inner)
    as32 = lambda a: jnp.asarray(a.astype(np.float32))
    return dict(
        first=as32(np.concatenate([np.cos(first), -np.sin(first)], 0)),
        turn_cos=as32(np.cos(turn))[:, None, :],
        turn_sin=as32(np.sin(turn))[:, None, :],
        inner=as32(np.block([[cos, -sin], [sin, cos]])),
        outer=as32(np.block([[cos, sin], [-sin, cos]])),
        last=as32(np.concatenate([weight * np.cos(first), -weight * np.sin(first)], 0).T),
        kept=kept,
    )


def forward_fourier(signal, tab):
    both = jnp.einsum("kn,ncm->kcm", tab["first"], signal, precision=exact)
    real, imag = both[: tab["kept"]], both[tab["kept"] :]
    turned = jnp.concatenate(
        [real * tab["turn_cos"] + imag * tab["turn_sin"], imag * tab["turn_cos"] - real * tab["turn_sin"]], 2
    )
    return jnp.einsum("kcm,mj->kcj", turned, tab["inner"], precision=exact)


def inverse_fourier(real, imag, tab):
    back = jnp.einsum("kcm,mj->kcj", jnp.concatenate([real, imag], 2), tab["outer"], precision=exact)
    real, imag = back[..., :side], back[..., side:]
    turned = jnp.concatenate(
        [real * tab["turn_cos"] - imag * tab["turn_sin"], imag * tab["turn_cos"] + real * tab["turn_sin"]], 0
    )
    return jnp.einsum("nk,kcm->ncm", tab["last"], turned, precision=exact)


def halves(spectrum):
    return spectrum[..., :side], spectrum[..., side:]


def across(block, target):
    pairs = []
    for h in range(2):
        for m in range(2):
            to_h, to_m = target(h, m)
            pairs.append((h * 2 + m, to_h * 2 + to_m))
    return lax.ppermute(block, ("h", "m"), pairs)


def other_h(block):
    return lax.ppermute(block, "h", [(0, 1), (1, 0)])


def tie(value, first):
    return value + 0.0 * first[(0,) * first.ndim]


def local(key_branch, value_branch, query_branch, long_filter, skip_weight, out_weight, cotangent):
    rows, chans = key_branch.shape
    n_ctx = 32
    group = chans // n_ctx
    seq_len = rows * n_ctx
    norm_scale = 1.0 / math.sqrt(seq_len)
    tab = tables(seq_len)
    at_h = lax.axis_index("h")
    at_m = lax.axis_index("m")
    at_ctx = lax.axis_index(CTX)

    weights = lax.all_gather(out_weight, PLANE, axis=1, tiled=True)

    cot_same = across(cotangent, lambda h, m: (m, h))
    cot_swap = across(cotangent, lambda h, m: (m, 1 - h))
    cot_pair = jnp.where(at_m == 0, jnp.stack([cot_same, cot_swap]), jnp.stack([cot_swap, cot_same]))

    product = key_branch * value_branch
    sent = jnp.concatenate(
        [product.T.reshape(n_ctx, group, rows), (long_filter * norm_scale).T.reshape(n_ctx, group, rows)], 1
    )
    signals = lax.all_to_all(sent, CTX, 0, 0)
    query_own = query_branch.T
    query_far = other_h(query_own)
    query_both = jnp.where(at_h == 0, jnp.stack([query_own, query_far]), jnp.stack([query_far, query_own]))

    cot_pair = tie(cot_pair, signals)
    cot_line = lax.all_to_all(jnp.broadcast_to(cot_pair[None], (4,) + cot_pair.shape), "l", 0, 0)

    spectra = forward_fourier(signals, tab)
    prod_real, prod_imag = halves(spectra[:, :group])
    taps_real, taps_imag = halves(spectra[:, group:])
    conv = inverse_fourier(
        prod_real * taps_real - prod_imag * taps_imag, prod_real * taps_imag + prod_imag * taps_real, tab
    )
    skip = lax.dynamic_slice(skip_weight, (at_ctx * group,), (group,))[None, :, None]
    chan_product = signals[:, :group]
    gate_chan = conv + skip * chan_product
    gate_chan = tie(tie(gate_chan, cot_line), weights)
    gate_pair = gate_chan.reshape(2, 16, group, rows).transpose(1, 0, 2, 3)
    gate_sent = jnp.broadcast_to(gate_pair[None], (2,) + gate_pair.shape).reshape(n_ctx, 2, group, rows)
    gate_got = lax.all_to_all(gate_sent, CTX, 0, 0)
    gate_both = gate_got.transpose(1, 0, 2, 3).reshape(2, chans, rows)
    mixed = query_both * gate_both
    mixed_flat = mixed.transpose(1, 0, 2).reshape(chans, 2 * rows)

    partial = lax.dot_general(
        mixed_flat, weights, (((0,), (0,)), ((), ())), precision=close, preferred_element_type=jnp.float32
    )
    partial = partial.reshape(2, rows, 4, 2, chans).transpose(3, 0, 2, 1, 4).reshape(2, 8, rows, chans)
    partial = lax.all_to_all(partial, "k", 0, 0).sum(0)
    projected = lax.psum_scatter(partial, LINE, scatter_dimension=0, tiled=False)
    projected = across(projected, lambda h, m: (m, h))

    cot_cores = lax.all_to_all(jnp.broadcast_to(cot_line[None], (2,) + cot_line.shape), "k", 0, 0)
    cot_full = (
        cot_cores.transpose(2, 3, 1, 0, 4).reshape(2 * rows, 8 * chans)
    )

    mixed_grad = lax.dot_general(
        weights, cot_full, (((1,), (1,)), ((), ())), precision=close, preferred_element_type=jnp.float32
    )
    mixed_grad = mixed_grad.reshape(chans, 2, rows).transpose(1, 0, 2)
    grad_sent = (mixed_grad * query_both).reshape(2, n_ctx, group, rows).transpose(1, 0, 2, 3)
    grad_got = lax.all_to_all(grad_sent, CTX, 0, 0)
    grad_chan = grad_got.reshape(2, 16, 2, group, rows).sum(0).transpose(1, 0, 2, 3).reshape(n_ctx, group, rows)

    own_grad = lax.dynamic_index_in_dim(mixed_grad, at_h, 0, False)
    far_grad = lax.dynamic_index_in_dim(mixed_grad, 1 - at_h, 0, False)
    own_gate = lax.dynamic_index_in_dim(gate_both, at_h, 0, False)
    query_grad = ((own_grad + other_h(far_grad)) * own_gate).T

    weight_part = lax.dot_general(
        mixed_flat, cot_full, (((1,), (0,)), ((), ())), precision=close, preferred_element_type=jnp.float32
    )
    weight_part = weight_part.reshape(chans, 16, rows).transpose(1, 0, 2)
    weight_grad = lax.all_to_all(weight_part, PLANE, 0, 0).sum(0) * norm_scale

    grad_real, grad_imag = halves(forward_fourier(grad_chan, tab))
    lead_real = jnp.concatenate([taps_real, prod_real], 1)
    lead_imag = jnp.concatenate([taps_imag, prod_imag], 1)
    grad_real = jnp.concatenate([grad_real, grad_real], 1)
    grad_imag = jnp.concatenate([grad_imag, grad_imag], 1)
    lagged = inverse_fourier(
        grad_real * lead_real + grad_imag * lead_imag, grad_imag * lead_real - grad_real * lead_imag, tab
    )
    prod_grad = lagged[:, :group] + skip * grad_chan
    skip_part = jnp.sum(grad_chan * chan_product, axis=(0, 2)) * norm_scale
    skip_row = jnp.broadcast_to(jnp.pad(skip_part, (0, rows - group))[None, None], (n_ctx, 1, rows))
    back = lax.all_to_all(jnp.concatenate([prod_grad, lagged[:, group:] * norm_scale, skip_row], 1), CTX, 0, 0)
    product_grad = back[:, :group].reshape(chans, rows).T
    filter_grad = back[:, group : 2 * group].reshape(chans, rows).T
    skip_grad = back[:, 2 * group, :group].reshape(chans)
    return (
        projected,
        product_grad * value_branch,
        product_grad * key_branch,
        query_grad,
        filter_grad,
        skip_grad,
        weight_grad,
    )


def solution(mesh):
    grid = Mesh(mesh.devices.reshape(SIZES), AXES)
    wide = P(("h", "y", "x"), ("m", "l", "k"))
    tall = P(("m", "l", "k"), ("h", "y", "x"))
    flat = P(("m", "l", "k"))
    return jax.shard_map(
        local,
        mesh=grid,
        in_specs=(wide, wide, wide, wide, flat, tall, wide),
        out_specs=(wide, wide, wide, wide, wide, flat, tall),
        check_vma=False,
    )
```

```python
import math

import jax
import jax.numpy as jnp
import numpy as np
from jax import lax
from jax.sharding import Mesh
from jax.sharding import PartitionSpec as P

AXES = ("h", "y", "x", "m", "l", "k")
SIZES = (2, 4, 4, 2, 4, 2)
CTX = ("h", "y", "x")
PLANE = ("y", "x")
LINE = ("m", "l")
side = 128
exact = lax.Precision.HIGHEST
close = lax.Precision.HIGH


def tables(seq_len):
    full = 2 * seq_len
    blocks = full // side
    kept = blocks // 2 + 1
    rows = np.arange(kept)
    first = 2.0 * np.pi * np.outer(rows, np.arange(seq_len // side)) / blocks
    turn = 2.0 * np.pi * np.outer(rows, np.arange(side)) / full
    inner = 2.0 * np.pi * np.outer(np.arange(side), np.arange(side)) / side
    weight = np.where((rows == 0) | (rows == blocks // 2), 1.0, 2.0)[:, None] / full
    cos, sin = np.cos(inner), np.sin(inner)
    as32 = lambda a: jnp.asarray(a.astype(np.float32))
    return dict(
        first=as32(np.concatenate([np.cos(first), -np.sin(first)], 0)),
        turn_cos=as32(np.cos(turn))[:, None, :],
        turn_sin=as32(np.sin(turn))[:, None, :],
        inner=as32(np.block([[cos, -sin], [sin, cos]])),
        outer=as32(np.block([[cos, sin], [-sin, cos]])),
        last=as32(np.concatenate([weight * np.cos(first), -weight * np.sin(first)], 0).T),
        kept=kept,
    )


def forward_fourier(signal, tab):
    both = jnp.einsum("kn,ncm->kcm", tab["first"], signal, precision=exact)
    real, imag = both[: tab["kept"]], both[tab["kept"] :]
    turned = jnp.concatenate(
        [real * tab["turn_cos"] + imag * tab["turn_sin"], imag * tab["turn_cos"] - real * tab["turn_sin"]], 2
    )
    return jnp.einsum("kcm,mj->kcj", turned, tab["inner"], precision=exact)


def inverse_fourier(real, imag, tab):
    back = jnp.einsum("kcm,mj->kcj", jnp.concatenate([real, imag], 2), tab["outer"], precision=exact)
    real, imag = back[..., :side], back[..., side:]
    turned = jnp.concatenate(
        [real * tab["turn_cos"] - imag * tab["turn_sin"], imag * tab["turn_cos"] + real * tab["turn_sin"]], 0
    )
    return jnp.einsum("nk,kcm->ncm", tab["last"], turned, precision=exact)


def halves(spectrum):
    return spectrum[..., :side], spectrum[..., side:]


def across(block, target):
    pairs = []
    for h in range(2):
        for m in range(2):
            to_h, to_m = target(h, m)
            pairs.append((h * 2 + m, to_h * 2 + to_m))
    return lax.ppermute(block, ("h", "m"), pairs)


def other_h(block):
    return lax.ppermute(block, "h", [(0, 1), (1, 0)])


def tie(value, first):
    return value + 0.0 * first[(0,) * first.ndim]


def local(key_branch, value_branch, query_branch, long_filter, skip_weight, out_weight, cotangent):
    rows, chans = key_branch.shape
    n_ctx = 32
    group = chans // n_ctx
    seq_len = rows * n_ctx
    norm_scale = 1.0 / math.sqrt(seq_len)
    tab = tables(seq_len)
    at_h = lax.axis_index("h")
    at_m = lax.axis_index("m")
    at_ctx = lax.axis_index(CTX)

    weights = lax.all_gather(out_weight, PLANE, axis=1, tiled=True)

    cot_same = across(cotangent, lambda h, m: (m, h))
    cot_swap = across(cotangent, lambda h, m: (m, 1 - h))
    cot_pair = jnp.where(at_m == 0, jnp.stack([cot_same, cot_swap]), jnp.stack([cot_swap, cot_same]))

    product = key_branch * value_branch
    sent = jnp.concatenate(
        [product.T.reshape(n_ctx, group, rows), (long_filter * norm_scale).T.reshape(n_ctx, group, rows)], 1
    )
    signals = lax.all_to_all(sent, CTX, 0, 0)
    query_own = query_branch.T
    query_far = other_h(query_own)
    query_both = jnp.where(at_h == 0, jnp.stack([query_own, query_far]), jnp.stack([query_far, query_own]))

    cot_pair = tie(cot_pair, signals)
    cot_line = lax.all_to_all(jnp.broadcast_to(cot_pair[None], (4,) + cot_pair.shape), "l", 0, 0)

    spectra = forward_fourier(signals, tab)
    prod_real, prod_imag = halves(spectra[:, :group])
    taps_real, taps_imag = halves(spectra[:, group:])
    conv = inverse_fourier(
        prod_real * taps_real - prod_imag * taps_imag, prod_real * taps_imag + prod_imag * taps_real, tab
    )
    skip = lax.dynamic_slice(skip_weight, (at_ctx * group,), (group,))[None, :, None]
    chan_product = signals[:, :group]
    gate_chan = conv + skip * chan_product
    gate_chan = tie(gate_chan, cot_line)
    gate_pair = gate_chan.reshape(2, 16, group, rows).transpose(1, 0, 2, 3)
    gate_sent = jnp.broadcast_to(gate_pair[None], (2,) + gate_pair.shape).reshape(n_ctx, 2, group, rows)
    gate_got = lax.all_to_all(gate_sent, CTX, 0, 0)
    gate_both = gate_got.transpose(1, 0, 2, 3).reshape(2, chans, rows)
    mixed = query_both * gate_both
    mixed_flat = mixed.transpose(1, 0, 2).reshape(chans, 2 * rows)

    partial = lax.dot_general(
        mixed_flat, weights, (((0,), (0,)), ((), ())), precision=close, preferred_element_type=jnp.float32
    )
    partial = partial.reshape(2, rows, 4, 2, chans).transpose(3, 0, 2, 1, 4).reshape(2, 8, rows, chans)
    partial = lax.all_to_all(partial, "k", 0, 0).sum(0)
    projected = lax.psum_scatter(partial, LINE, scatter_dimension=0, tiled=False)
    cot_line = tie(cot_line, gate_got)
    cot_cores = lax.all_to_all(jnp.broadcast_to(cot_line[None], (2,) + cot_line.shape), "k", 0, 0)
    cot_full = (
        cot_cores.transpose(2, 3, 1, 0, 4).reshape(2 * rows, 8 * chans)
    )

    mixed_grad = lax.dot_general(
        weights, cot_full, (((1,), (1,)), ((), ())), precision=close, preferred_element_type=jnp.float32
    )
    mixed_grad = mixed_grad.reshape(chans, 2, rows).transpose(1, 0, 2)
    grad_sent = tie(mixed_grad * query_both, partial).reshape(2, n_ctx, group, rows).transpose(1, 0, 2, 3)
    grad_got = lax.all_to_all(grad_sent, CTX, 0, 0)
    grad_chan = grad_got.reshape(2, 16, 2, group, rows).sum(0).transpose(1, 0, 2, 3).reshape(n_ctx, group, rows)

    own_grad = lax.dynamic_index_in_dim(mixed_grad, at_h, 0, False)
    far_grad = lax.dynamic_index_in_dim(mixed_grad, 1 - at_h, 0, False)
    own_gate = lax.dynamic_index_in_dim(gate_both, at_h, 0, False)
    far_grad = other_h(far_grad)
    query_grad = ((own_grad + far_grad) * own_gate).T

    weight_part = lax.dot_general(
        mixed_flat, cot_full, (((1,), (0,)), ((), ())), precision=close, preferred_element_type=jnp.float32
    )
    weight_part = weight_part.reshape(chans, 16, rows).transpose(1, 0, 2)
    weight_grad = lax.all_to_all(weight_part, PLANE, 0, 0).sum(0) * norm_scale

    grad_real, grad_imag = halves(forward_fourier(grad_chan, tab))
    lead_real = jnp.concatenate([taps_real, prod_real], 1)
    lead_imag = jnp.concatenate([taps_imag, prod_imag], 1)
    grad_real = jnp.concatenate([grad_real, grad_real], 1)
    grad_imag = jnp.concatenate([grad_imag, grad_imag], 1)
    lagged = inverse_fourier(
        grad_real * lead_real + grad_imag * lead_imag, grad_imag * lead_real - grad_real * lead_imag, tab
    )
    prod_grad = lagged[:, :group] + skip * grad_chan
    skip_part = jnp.sum(grad_chan * chan_product, axis=(0, 2)) * norm_scale
    skip_row = jnp.broadcast_to(jnp.pad(skip_part, (0, rows - group))[None, None], (n_ctx, 1, rows))
    back_sent = jnp.concatenate([tie(tie(tie(prod_grad, weight_grad), projected), far_grad), lagged[:, group:] * norm_scale, skip_row], 1)
    back = lax.all_to_all(back_sent, CTX, 0, 0)
    projected = across(projected, lambda h, m: (m, h))
    product_grad = back[:, :group].reshape(chans, rows).T
    filter_grad = back[:, group : 2 * group].reshape(chans, rows).T
    skip_grad = back[:, 2 * group, :group].reshape(chans)
    return (
        projected,
        product_grad * value_branch,
        product_grad * key_branch,
        query_grad,
        filter_grad,
        skip_grad,
        weight_grad,
    )


def solution(mesh):
    grid = Mesh(mesh.devices.reshape(SIZES), AXES)
    wide = P(("h", "y", "x"), ("m", "l", "k"))
    tall = P(("m", "l", "k"), ("h", "y", "x"))
    flat = P(("m", "l", "k"))
    return jax.shard_map(
        local,
        mesh=grid,
        in_specs=(wide, wide, wide, wide, flat, tall, wide),
        out_specs=(wide, wide, wide, wide, wide, flat, tall),
        check_vma=False,
    )
```

```python
import math

import jax
import jax.numpy as jnp
import numpy as np
from jax import lax
from jax.sharding import Mesh
from jax.sharding import PartitionSpec as P

AXES = ("h", "y", "x", "m", "l", "k")
SIZES = (2, 4, 4, 2, 4, 2)
CTX = ("h", "y", "x")
PLANE = ("y", "x")
LINE = ("m", "l")
side = 128
exact = lax.Precision.HIGHEST
close = lax.Precision.HIGH


def tables(seq_len):
    full = 2 * seq_len
    blocks = full // side
    kept = blocks // 2 + 1
    rows = np.arange(kept)
    first = 2.0 * np.pi * np.outer(rows, np.arange(seq_len // side)) / blocks
    turn = 2.0 * np.pi * np.outer(rows, np.arange(side)) / full
    inner = 2.0 * np.pi * np.outer(np.arange(side), np.arange(side)) / side
    weight = np.where((rows == 0) | (rows == blocks // 2), 1.0, 2.0)[:, None] / full
    cos, sin = np.cos(inner), np.sin(inner)
    as32 = lambda a: jnp.asarray(a.astype(np.float32))
    return dict(
        first=as32(np.concatenate([np.cos(first), -np.sin(first)], 0)),
        turn_cos=as32(np.cos(turn))[:, None, :],
        turn_sin=as32(np.sin(turn))[:, None, :],
        inner=as32(np.block([[cos, -sin], [sin, cos]])),
        outer=as32(np.block([[cos, sin], [-sin, cos]])),
        last=as32(np.concatenate([weight * np.cos(first), -weight * np.sin(first)], 0).T),
        kept=kept,
    )


def forward_fourier(signal, tab):
    both = jnp.einsum("kn,ncm->kcm", tab["first"], signal, precision=exact)
    real, imag = both[: tab["kept"]], both[tab["kept"] :]
    turned = jnp.concatenate(
        [real * tab["turn_cos"] + imag * tab["turn_sin"], imag * tab["turn_cos"] - real * tab["turn_sin"]], 2
    )
    return jnp.einsum("kcm,mj->kcj", turned, tab["inner"], precision=exact)


def inverse_fourier(real, imag, tab):
    back = jnp.einsum("kcm,mj->kcj", jnp.concatenate([real, imag], 2), tab["outer"], precision=exact)
    real, imag = back[..., :side], back[..., side:]
    turned = jnp.concatenate(
        [real * tab["turn_cos"] - imag * tab["turn_sin"], imag * tab["turn_cos"] + real * tab["turn_sin"]], 0
    )
    return jnp.einsum("nk,kcm->ncm", tab["last"], turned, precision=exact)


def halves(spectrum):
    return spectrum[..., :side], spectrum[..., side:]


def across(block, target):
    pairs = []
    for h in range(2):
        for m in range(2):
            to_h, to_m = target(h, m)
            pairs.append((h * 2 + m, to_h * 2 + to_m))
    return lax.ppermute(block, ("h", "m"), pairs)


def other_h(block):
    return lax.ppermute(block, "h", [(0, 1), (1, 0)])


def tie(value, first):
    return value + 0.0 * first[(0,) * first.ndim]


def local(key_branch, value_branch, query_branch, long_filter, skip_weight, out_weight, cotangent):
    rows, chans = key_branch.shape
    n_ctx = 32
    group = chans // n_ctx
    seq_len = rows * n_ctx
    norm_scale = 1.0 / math.sqrt(seq_len)
    tab = tables(seq_len)
    at_h = lax.axis_index("h")
    at_ctx = lax.axis_index(CTX)

    cot_mine = across(cotangent, lambda h, m: (m, h))
    cot_line = lax.all_gather(cot_mine, LINE, axis=0)

    query_own = query_branch.T
    query_far = other_h(query_own)
    query_both = jnp.where(at_h == 0, jnp.stack([query_own, query_far]), jnp.stack([query_far, query_own]))

    weights = lax.all_to_all(jnp.broadcast_to(out_weight[None], (16,) + out_weight.shape), PLANE, 0, 0)

    product = key_branch * value_branch
    sent = jnp.concatenate(
        [product.T.reshape(n_ctx, group, rows), (long_filter * norm_scale).T.reshape(n_ctx, group, rows)], 1
    )
    sent = tie(tie(tie(sent, weights), query_far), cot_mine)
    signals = lax.all_to_all(sent, CTX, 0, 0)
    weights = weights.transpose(1, 0, 2).reshape(chans, -1)

    spectra = forward_fourier(signals, tab)
    prod_real, prod_imag = halves(spectra[:, :group])
    taps_real, taps_imag = halves(spectra[:, group:])
    conv = inverse_fourier(
        prod_real * taps_real - prod_imag * taps_imag, prod_real * taps_imag + prod_imag * taps_real, tab
    )
    skip = lax.dynamic_slice(skip_weight, (at_ctx * group,), (group,))[None, :, None]
    chan_product = signals[:, :group]
    gate_chan = conv + skip * chan_product
    gate_pair = gate_chan.reshape(2, 16, group, rows).transpose(1, 0, 2, 3)
    gate_sent = jnp.broadcast_to(gate_pair[None], (2,) + gate_pair.shape).reshape(n_ctx, 2, group, rows)
    gate_got = lax.all_to_all(gate_sent, CTX, 0, 0)
    gate_both = gate_got.transpose(1, 0, 2, 3).reshape(2, chans, rows)
    mixed = query_both * gate_both
    mixed_flat = mixed.transpose(1, 0, 2).reshape(chans, 2 * rows)

    partial = lax.dot_general(
        mixed_flat, weights, (((0,), (0,)), ((), ())), precision=close, preferred_element_type=jnp.float32
    )
    partial = partial.reshape(2, rows, 4, 2, chans).transpose(3, 0, 2, 1, 4).reshape(2, 8, rows, chans)
    partial = lax.all_to_all(partial, "k", 0, 0).sum(0)
    projected = lax.psum_scatter(partial, LINE, scatter_dimension=0, tiled=False)
    cot_line = tie(cot_line, partial)
    cot_cores = lax.all_to_all(jnp.broadcast_to(cot_line[None], (2,) + cot_line.shape), "k", 0, 0)
    cot_full = (
        cot_cores.reshape(2, 2, 4, rows, chans).transpose(1, 3, 2, 0, 4).reshape(2 * rows, 8 * chans)
    )

    mixed_grad = lax.dot_general(
        weights, cot_full, (((1,), (1,)), ((), ())), precision=close, preferred_element_type=jnp.float32
    )
    mixed_grad = mixed_grad.reshape(chans, 2, rows).transpose(1, 0, 2)
    grad_sent = (mixed_grad * query_both).reshape(2, n_ctx, group, rows).transpose(1, 0, 2, 3)
    grad_got = lax.all_to_all(grad_sent, CTX, 0, 0)
    grad_chan = grad_got.reshape(2, 16, 2, group, rows).sum(0).transpose(1, 0, 2, 3).reshape(n_ctx, group, rows)

    own_grad = lax.dynamic_index_in_dim(mixed_grad, at_h, 0, False)
    far_grad = lax.dynamic_index_in_dim(mixed_grad, 1 - at_h, 0, False)
    own_gate = lax.dynamic_index_in_dim(gate_both, at_h, 0, False)
    far_grad = other_h(tie(far_grad, grad_got))
    query_grad = ((own_grad + far_grad) * own_gate).T

    weight_part = lax.dot_general(
        mixed_flat, cot_full, (((1,), (0,)), ((), ())), precision=close, preferred_element_type=jnp.float32
    )
    weight_part = weight_part.reshape(chans, 16, rows).transpose(1, 0, 2)
    weight_grad = lax.all_to_all(weight_part, PLANE, 0, 0).sum(0) * norm_scale

    grad_real, grad_imag = halves(forward_fourier(grad_chan, tab))
    lead_real = jnp.concatenate([taps_real, prod_real], 1)
    lead_imag = jnp.concatenate([taps_imag, prod_imag], 1)
    grad_real = jnp.concatenate([grad_real, grad_real], 1)
    grad_imag = jnp.concatenate([grad_imag, grad_imag], 1)
    lagged = inverse_fourier(
        grad_real * lead_real + grad_imag * lead_imag, grad_imag * lead_real - grad_real * lead_imag, tab
    )
    prod_grad = lagged[:, :group] + skip * grad_chan
    skip_part = jnp.sum(grad_chan * chan_product, axis=(0, 2)) * norm_scale
    skip_row = jnp.broadcast_to(jnp.pad(skip_part, (0, rows - group))[None, None], (n_ctx, 1, rows))
    back_sent = jnp.concatenate([tie(tie(tie(prod_grad, weight_grad), projected), far_grad), lagged[:, group:] * norm_scale, skip_row], 1)
    back = lax.all_to_all(back_sent, CTX, 0, 0)
    projected = across(projected, lambda h, m: (m, h))
    product_grad = back[:, :group].reshape(chans, rows).T
    filter_grad = back[:, group : 2 * group].reshape(chans, rows).T
    skip_grad = back[:, 2 * group, :group].reshape(chans)
    return (
        projected,
        product_grad * value_branch,
        product_grad * key_branch,
        query_grad,
        filter_grad,
        skip_grad,
        weight_grad,
    )


def solution(mesh):
    grid = Mesh(mesh.devices.reshape(SIZES), AXES)
    wide = P(("h", "y", "x"), ("m", "l", "k"))
    tall = P(("m", "l", "k"), ("h", "y", "x"))
    flat = P(("m", "l", "k"))
    return jax.shard_map(
        local,
        mesh=grid,
        in_specs=(wide, wide, wide, wide, flat, tall, wide),
        out_specs=(wide, wide, wide, wide, wide, flat, tall),
        check_vma=False,
    )
```

```python
import math

import jax
import jax.numpy as jnp
import numpy as np
from jax import lax
from jax.sharding import Mesh
from jax.sharding import PartitionSpec as P

AXES = ("h", "y", "x", "m", "l", "k")
SIZES = (2, 4, 4, 2, 4, 2)
CTX = ("h", "y", "x")
PLANE = ("y", "x")
LINE = ("m", "l")
side = 128
exact = lax.Precision.HIGHEST
close = lax.Precision.HIGH


def tables(seq_len):
    full = 2 * seq_len
    blocks = full // side
    kept = blocks // 2 + 1
    rows = np.arange(kept)
    first = 2.0 * np.pi * np.outer(rows, np.arange(seq_len // side)) / blocks
    turn = 2.0 * np.pi * np.outer(rows, np.arange(side)) / full
    inner = 2.0 * np.pi * np.outer(np.arange(side), np.arange(side)) / side
    weight = np.where((rows == 0) | (rows == blocks // 2), 1.0, 2.0)[:, None] / full
    cos, sin = np.cos(inner), np.sin(inner)
    as32 = lambda a: jnp.asarray(a.astype(np.float32))
    return dict(
        first=as32(np.concatenate([np.cos(first), -np.sin(first)], 0)),
        turn_cos=as32(np.cos(turn))[:, None, :],
        turn_sin=as32(np.sin(turn))[:, None, :],
        inner=as32(np.block([[cos, -sin], [sin, cos]])),
        outer=as32(np.block([[cos, sin], [-sin, cos]])),
        last=as32(np.concatenate([weight * np.cos(first), -weight * np.sin(first)], 0).T),
        kept=kept,
    )


def forward_fourier(signal, tab):
    both = jnp.einsum("kn,ncm->kcm", tab["first"], signal, precision=exact)
    real, imag = both[: tab["kept"]], both[tab["kept"] :]
    turned = jnp.concatenate(
        [real * tab["turn_cos"] + imag * tab["turn_sin"], imag * tab["turn_cos"] - real * tab["turn_sin"]], 2
    )
    return jnp.einsum("kcm,mj->kcj", turned, tab["inner"], precision=exact)


def inverse_fourier(real, imag, tab):
    back = jnp.einsum("kcm,mj->kcj", jnp.concatenate([real, imag], 2), tab["outer"], precision=exact)
    real, imag = back[..., :side], back[..., side:]
    turned = jnp.concatenate(
        [real * tab["turn_cos"] - imag * tab["turn_sin"], imag * tab["turn_cos"] + real * tab["turn_sin"]], 0
    )
    return jnp.einsum("nk,kcm->ncm", tab["last"], turned, precision=exact)


def halves(spectrum):
    return spectrum[..., :side], spectrum[..., side:]


def across(block, target):
    pairs = []
    for h in range(2):
        for m in range(2):
            to_h, to_m = target(h, m)
            pairs.append((h * 2 + m, to_h * 2 + to_m))
    return lax.ppermute(block, ("h", "m"), pairs)


def other_h(block):
    return lax.ppermute(block, "h", [(0, 1), (1, 0)])


def other_core(block):
    return lax.ppermute(block, "k", [(0, 1), (1, 0)])


def in_order(own, other, at):
    return jnp.where(at == 0, jnp.stack([own, other]), jnp.stack([other, own]))


def tie(value, *first):
    for array in first:
        value = value + 0.0 * array[(0,) * array.ndim]
    return value


def pick(pair, at):
    return lax.dynamic_index_in_dim(pair, at, 0, False)


def product_of(left, right, left_dim, right_dim):
    return lax.dot_general(
        left, right, (((left_dim,), (right_dim,)), ((), ())), precision=close, preferred_element_type=jnp.float32
    )


def local(key_branch, value_branch, query_branch, long_filter, skip_weight, out_weight, cotangent):
    rows, chans = key_branch.shape
    n_ctx = 32
    group = chans // n_ctx
    seq_len = rows * n_ctx
    norm_scale = 1.0 / math.sqrt(seq_len)
    tab = tables(seq_len)
    at_h, at_m, at_k = (lax.axis_index(name) for name in ("h", "m", "k"))
    at_ctx = lax.axis_index(CTX)

    weights = lax.all_gather(out_weight, PLANE, axis=1, tiled=True)

    cot_same = across(cotangent, lambda h, m: (m, h))
    cot_swap = across(cotangent, lambda h, m: (m, 1 - h))
    cot_pair = in_order(cot_same, cot_swap, at_m)

    product = key_branch * value_branch
    sent = jnp.concatenate(
        [product.T.reshape(n_ctx, group, rows), (long_filter * norm_scale).T.reshape(n_ctx, group, rows)], 1
    )
    signals = lax.all_to_all(sent, CTX, 0, 0)
    query_own = query_branch.T
    query_far = other_h(tie(query_own, signals))
    query_both = in_order(query_own, query_far, at_h)

    cot_pair = tie(cot_pair, signals)
    cot_line = lax.all_to_all(jnp.broadcast_to(cot_pair[None], (4,) + cot_pair.shape), "l", 0, 0)
    cot_cores = in_order(cot_line, other_core(cot_line), at_k)
    cot_full = cot_cores.transpose(2, 3, 1, 0, 4).reshape(2 * rows, 8 * chans)

    spectra = forward_fourier(signals, tab)
    prod_real, prod_imag = halves(spectra[:, :group])
    taps_real, taps_imag = halves(spectra[:, group:])
    conv = inverse_fourier(
        prod_real * taps_real - prod_imag * taps_imag, prod_real * taps_imag + prod_imag * taps_real, tab
    )
    skip = lax.dynamic_slice(skip_weight, (at_ctx * group,), (group,))[None, :, None]
    chan_product = signals[:, :group]
    gate_chan = conv + skip * chan_product
    gate_chan = tie(gate_chan, cot_line, weights, query_far)
    gate_pair = gate_chan.reshape(2, 16, group, rows).transpose(1, 0, 2, 3)
    gate_sent = jnp.broadcast_to(gate_pair[None], (2,) + gate_pair.shape).reshape(n_ctx, 2, group, rows)
    gate_got = lax.all_to_all(gate_sent, CTX, 0, 0)

    mixed_grad = product_of(weights, cot_full, 1, 1)
    mixed_grad = mixed_grad.reshape(chans, 2, rows).transpose(1, 0, 2)
    grad_sent = (mixed_grad * query_both).reshape(2, n_ctx, group, rows).transpose(1, 0, 2, 3)
    gate_got = tie(gate_got, grad_sent)
    grad_got = lax.all_to_all(tie(grad_sent, gate_got), CTX, 0, 0)

    gate_both = gate_got.transpose(1, 0, 2, 3).reshape(2, chans, rows)
    mixed = query_both * gate_both
    mixed_flat = mixed.transpose(1, 0, 2).reshape(chans, 2 * rows)
    grad_chan = grad_got.reshape(2, 16, 2, group, rows).sum(0).transpose(1, 0, 2, 3).reshape(n_ctx, group, rows)

    weight_part = product_of(mixed_flat, cot_full, 1, 0)
    weight_part = weight_part.reshape(chans, 16, rows).transpose(1, 0, 2)
    weight_grad = lax.psum_scatter(weight_part, "y", scatter_dimension=0, tiled=True)
    weight_grad = lax.psum_scatter(weight_grad, "x", scatter_dimension=0, tiled=False) * norm_scale

    partial = product_of(mixed_flat, weights, 0, 0)
    partial = partial.reshape(2, rows, 4, 2, chans).transpose(3, 2, 0, 1, 4)
    partial = pick(partial, at_k) + other_core(pick(partial, 1 - at_k))
    partial = lax.all_to_all(tie(partial, grad_got), "l", 0, 0).sum(0)
    projected = across(pick(partial, at_m), lambda h, m: (m, h))
    projected = projected + across(pick(partial, 1 - at_m), lambda h, m: (1 - m, h))

    far_grad = other_h(tie(pick(mixed_grad, 1 - at_h), grad_got))
    query_grad = ((pick(mixed_grad, at_h) + far_grad) * pick(gate_both, at_h)).T

    grad_real, grad_imag = halves(forward_fourier(grad_chan, tab))
    lead_real = jnp.concatenate([taps_real, prod_real], 1)
    lead_imag = jnp.concatenate([taps_imag, prod_imag], 1)
    grad_real = jnp.concatenate([grad_real, grad_real], 1)
    grad_imag = jnp.concatenate([grad_imag, grad_imag], 1)
    lagged = inverse_fourier(
        grad_real * lead_real + grad_imag * lead_imag, grad_imag * lead_real - grad_real * lead_imag, tab
    )
    prod_grad = tie(lagged[:, :group] + skip * grad_chan, partial, far_grad)
    skip_part = jnp.sum(grad_chan * chan_product, axis=(0, 2)) * norm_scale
    skip_row = jnp.broadcast_to(jnp.pad(skip_part, (0, rows - group))[None, None], (n_ctx, 1, rows))
    back = lax.all_to_all(jnp.concatenate([prod_grad, lagged[:, group:] * norm_scale, skip_row], 1), CTX, 0, 0)
    product_grad = back[:, :group].reshape(chans, rows).T
    filter_grad = back[:, group : 2 * group].reshape(chans, rows).T
    skip_grad = back[:, 2 * group, :group].reshape(chans)
    return (
        projected,
        product_grad * value_branch,
        product_grad * key_branch,
        query_grad,
        filter_grad,
        skip_grad,
        weight_grad,
    )


def solution(mesh):
    grid = Mesh(mesh.devices.reshape(SIZES), AXES)
    wide = P(("h", "y", "x"), ("m", "l", "k"))
    tall = P(("m", "l", "k"), ("h", "y", "x"))
    flat = P(("m", "l", "k"))
    return jax.shard_map(
        local,
        mesh=grid,
        in_specs=(wide, wide, wide, wide, flat, tall, wide),
        out_specs=(wide, wide, wide, wide, wide, flat, tall),
        check_vma=False,
    )
```

```python
import math

import jax
import jax.numpy as jnp
import numpy as np
from jax import lax
from jax.sharding import Mesh
from jax.sharding import PartitionSpec as P

AXES = ("h", "y", "x", "m", "l", "k")
SIZES = (2, 4, 4, 2, 4, 2)
CTX = ("h", "y", "x")
PLANE = ("y", "x")
LINE = ("m", "l")
side = 128
exact = lax.Precision.HIGHEST
close = lax.Precision.HIGH


def tables(seq_len):
    full = 2 * seq_len
    blocks = full // side
    kept = blocks // 2 + 1
    rows = np.arange(kept)
    first = 2.0 * np.pi * np.outer(rows, np.arange(seq_len // side)) / blocks
    turn = 2.0 * np.pi * np.outer(rows, np.arange(side)) / full
    inner = 2.0 * np.pi * np.outer(np.arange(side), np.arange(side)) / side
    weight = np.where((rows == 0) | (rows == blocks // 2), 1.0, 2.0)[:, None] / full
    cos, sin = np.cos(inner), np.sin(inner)
    as32 = lambda a: jnp.asarray(a.astype(np.float32))
    return dict(
        first=as32(np.concatenate([np.cos(first), -np.sin(first)], 0)),
        turn_cos=as32(np.cos(turn))[:, None, :],
        turn_sin=as32(np.sin(turn))[:, None, :],
        inner=as32(np.block([[cos, -sin], [sin, cos]])),
        outer=as32(np.block([[cos, sin], [-sin, cos]])),
        last=as32(np.concatenate([weight * np.cos(first), -weight * np.sin(first)], 0).T),
        kept=kept,
    )


def forward_fourier(signal, tab):
    both = jnp.einsum("kn,ncm->kcm", tab["first"], signal, precision=exact)
    real, imag = both[: tab["kept"]], both[tab["kept"] :]
    turned = jnp.concatenate(
        [real * tab["turn_cos"] + imag * tab["turn_sin"], imag * tab["turn_cos"] - real * tab["turn_sin"]], 2
    )
    return jnp.einsum("kcm,mj->kcj", turned, tab["inner"], precision=exact)


def inverse_fourier(real, imag, tab):
    back = jnp.einsum("kcm,mj->kcj", jnp.concatenate([real, imag], 2), tab["outer"], precision=exact)
    real, imag = back[..., :side], back[..., side:]
    turned = jnp.concatenate(
        [real * tab["turn_cos"] - imag * tab["turn_sin"], imag * tab["turn_cos"] + real * tab["turn_sin"]], 0
    )
    return jnp.einsum("nk,kcm->ncm", tab["last"], turned, precision=exact)


def halves(spectrum):
    return spectrum[..., :side], spectrum[..., side:]


def across(block, target):
    pairs = []
    for h in range(2):
        for m in range(2):
            to_h, to_m = target(h, m)
            pairs.append((h * 2 + m, to_h * 2 + to_m))
    return lax.ppermute(block, ("h", "m"), pairs)


def other_core(block):
    return lax.ppermute(block, "k", [(0, 1), (1, 0)])


def in_order(own, other, at):
    return jnp.where(at == 0, jnp.stack([own, other]), jnp.stack([other, own]))


def tie(value, *first):
    for array in first:
        value = value + 0.0 * array[(0,) * array.ndim]
    return value


def pick(pair, at):
    return lax.dynamic_index_in_dim(pair, at, 0, False)


def product_of(left, right, left_dim, right_dim):
    return lax.dot_general(
        left, right, (((left_dim,), (right_dim,)), ((), ())), precision=close, preferred_element_type=jnp.float32
    )


def local(key_branch, value_branch, query_branch, long_filter, skip_weight, out_weight, cotangent):
    rows, chans = key_branch.shape
    n_ctx = 32
    group = chans // n_ctx
    seq_len = rows * n_ctx
    norm_scale = 1.0 / math.sqrt(seq_len)
    tab = tables(seq_len)
    at_m, at_k = (lax.axis_index(name) for name in ("m", "k"))
    at_ctx = lax.axis_index(CTX)

    weights = lax.all_gather(out_weight, PLANE, axis=1, tiled=True)

    cot_same = across(cotangent, lambda h, m: (m, h))
    cot_swap = across(cotangent, lambda h, m: (m, 1 - h))
    cot_pair = in_order(cot_same, cot_swap, at_m)

    sent = [key_branch * value_branch, long_filter * norm_scale, query_branch]
    sent = jnp.concatenate([array.T.reshape(n_ctx, group, rows) for array in sent], 1)
    signals = lax.all_to_all(sent, CTX, 0, 0)
    product, query = signals[:, :group], signals[:, 2 * group :]

    cot_pair = tie(cot_pair, signals)
    cot_line = lax.all_to_all(jnp.broadcast_to(cot_pair[None], (4,) + cot_pair.shape), "l", 0, 0)
    cot_cores = in_order(cot_line, other_core(cot_line), at_k)
    cot_full = cot_cores.transpose(2, 3, 1, 0, 4).reshape(2 * rows, 8 * chans)

    spectra = forward_fourier(signals[:, : 2 * group], tab)
    prod_real, prod_imag = halves(spectra[:, :group])
    taps_real, taps_imag = halves(spectra[:, group:])
    conv = inverse_fourier(
        prod_real * taps_real - prod_imag * taps_imag, prod_real * taps_imag + prod_imag * taps_real, tab
    )
    skip = lax.dynamic_slice(skip_weight, (at_ctx * group,), (group,))[None, :, None]
    gate = conv + skip * product
    mixed = tie(gate * query, cot_line, weights)
    mixed = mixed.reshape(2, 16, group, rows).transpose(1, 0, 2, 3)
    mixed = jnp.broadcast_to(mixed[None], (2,) + mixed.shape).reshape(n_ctx, 2, group, rows)
    mixed = lax.all_to_all(mixed, CTX, 0, 0)

    mixed_grad = product_of(weights, cot_full, 1, 1)
    mixed_grad = mixed_grad.reshape(n_ctx, group, 2, rows).transpose(0, 2, 1, 3)
    mixed = tie(mixed, mixed_grad)
    grad = lax.all_to_all(tie(mixed_grad, mixed), CTX, 0, 0)
    grad = grad.reshape(2, 16, 2, group, rows).sum(0).transpose(1, 0, 2, 3).reshape(n_ctx, group, rows)
    pre_grad = grad * query
    mixed = mixed.transpose(0, 2, 1, 3).reshape(chans, 2 * rows)

    weight_part = product_of(mixed, cot_full, 1, 0)
    weight_part = weight_part.reshape(chans, 16, rows).transpose(1, 0, 2)
    weight_grad = lax.psum_scatter(weight_part, "y", scatter_dimension=0, tiled=True)
    weight_grad = lax.psum_scatter(weight_grad, "x", scatter_dimension=0, tiled=False) * norm_scale

    partial = product_of(mixed, weights, 0, 0)
    partial = partial.reshape(2, rows, 4, 2, chans).transpose(3, 2, 0, 1, 4)
    partial = pick(partial, at_k) + other_core(pick(partial, 1 - at_k))
    partial = lax.all_to_all(tie(partial, grad), "l", 0, 0).sum(0)
    projected = across(pick(partial, at_m), lambda h, m: (m, h))
    projected = projected + across(pick(partial, 1 - at_m), lambda h, m: (1 - m, h))

    grad_real, grad_imag = halves(forward_fourier(pre_grad, tab))
    lead_real = jnp.concatenate([taps_real, prod_real], 1)
    lead_imag = jnp.concatenate([taps_imag, prod_imag], 1)
    grad_real = jnp.concatenate([grad_real, grad_real], 1)
    grad_imag = jnp.concatenate([grad_imag, grad_imag], 1)
    lagged = inverse_fourier(
        grad_real * lead_real + grad_imag * lead_imag, grad_imag * lead_real - grad_real * lead_imag, tab
    )
    prod_grad = tie(lagged[:, :group] + skip * pre_grad, partial)
    skip_part = jnp.sum(pre_grad * product, axis=(0, 2)) * norm_scale
    skip_row = jnp.broadcast_to(jnp.pad(skip_part, (0, rows - group))[None, None], (n_ctx, 1, rows))
    back = [prod_grad, lagged[:, group:] * norm_scale, grad * gate, skip_row]
    back = lax.all_to_all(jnp.concatenate(back, 1), CTX, 0, 0)
    product_grad, filter_grad, query_grad = (
        back[:, at * group : (at + 1) * group].reshape(chans, rows).T for at in range(3)
    )
    skip_grad = back[:, 3 * group, :group].reshape(chans)
    return (
        projected,
        product_grad * value_branch,
        product_grad * key_branch,
        query_grad,
        filter_grad,
        skip_grad,
        weight_grad,
    )


def solution(mesh):
    grid = Mesh(mesh.devices.reshape(SIZES), AXES)
    wide = P(("h", "y", "x"), ("m", "l", "k"))
    tall = P(("m", "l", "k"), ("h", "y", "x"))
    flat = P(("m", "l", "k"))
    return jax.shard_map(
        local,
        mesh=grid,
        in_specs=(wide, wide, wide, wide, flat, tall, wide),
        out_specs=(wide, wide, wide, wide, wide, flat, tall),
        check_vma=False,
    )
```

```python
import math

import jax
import jax.numpy as jnp
import numpy as np
from jax import lax
from jax.sharding import Mesh
from jax.sharding import PartitionSpec as P

AXES = ("h", "y", "x", "m", "l", "k")
SIZES = (2, 4, 4, 2, 4, 2)
CTX = ("h", "y", "x")
PLANE = ("y", "x")
LINE = ("m", "l")
side = 128
exact = lax.Precision.HIGHEST
close = lax.Precision.HIGH


def tables(seq_len):
    full = 2 * seq_len
    blocks = full // side
    kept = blocks // 2 + 1
    rows = np.arange(kept)
    first = 2.0 * np.pi * np.outer(rows, np.arange(seq_len // side)) / blocks
    turn = 2.0 * np.pi * np.outer(rows, np.arange(side)) / full
    inner = 2.0 * np.pi * np.outer(np.arange(side), np.arange(side)) / side
    weight = np.where((rows == 0) | (rows == blocks // 2), 1.0, 2.0)[:, None] / full
    cos, sin = np.cos(inner), np.sin(inner)
    as32 = lambda a: jnp.asarray(a.astype(np.float32))
    return dict(
        first=as32(np.concatenate([np.cos(first), -np.sin(first)], 0)),
        turn_cos=as32(np.cos(turn))[:, None, :],
        turn_sin=as32(np.sin(turn))[:, None, :],
        inner=as32(np.block([[cos, -sin], [sin, cos]])),
        outer=as32(np.block([[cos, sin], [-sin, cos]])),
        last=as32(np.concatenate([weight * np.cos(first), -weight * np.sin(first)], 0).T),
        kept=kept,
    )


def forward_fourier(signal, tab):
    both = jnp.einsum("kn,ncm->kcm", tab["first"], signal, precision=exact)
    real, imag = both[: tab["kept"]], both[tab["kept"] :]
    turned = jnp.concatenate(
        [real * tab["turn_cos"] + imag * tab["turn_sin"], imag * tab["turn_cos"] - real * tab["turn_sin"]], 2
    )
    return jnp.einsum("kcm,mj->kcj", turned, tab["inner"], precision=exact)


def inverse_fourier(real, imag, tab):
    back = jnp.einsum("kcm,mj->kcj", jnp.concatenate([real, imag], 2), tab["outer"], precision=exact)
    real, imag = back[..., :side], back[..., side:]
    turned = jnp.concatenate(
        [real * tab["turn_cos"] - imag * tab["turn_sin"], imag * tab["turn_cos"] + real * tab["turn_sin"]], 0
    )
    return jnp.einsum("nk,kcm->ncm", tab["last"], turned, precision=exact)


def halves(spectrum):
    return spectrum[..., :side], spectrum[..., side:]


def across(block, target):
    pairs = []
    for h in range(2):
        for m in range(2):
            to_h, to_m = target(h, m)
            pairs.append((h * 2 + m, to_h * 2 + to_m))
    return lax.ppermute(block, ("h", "m"), pairs)


def other_core(block):
    return lax.ppermute(block, "k", [(0, 1), (1, 0)])


def in_order(own, other, at):
    return jnp.where(at == 0, jnp.stack([own, other]), jnp.stack([other, own]))


def tie(value, *first):
    for array in first:
        value = value + 0.0 * array[(0,) * array.ndim]
    return value


def pick(pair, at):
    return lax.dynamic_index_in_dim(pair, at, 0, False)


def product_of(left, right, left_dim, right_dim):
    return lax.dot_general(
        left, right, (((left_dim,), (right_dim,)), ((), ())), precision=close, preferred_element_type=jnp.float32
    )


def local(key_branch, value_branch, query_branch, long_filter, skip_weight, out_weight, cotangent):
    rows, chans = key_branch.shape
    n_ctx = 32
    group = chans // n_ctx
    seq_len = rows * n_ctx
    norm_scale = 1.0 / math.sqrt(seq_len)
    tab = tables(seq_len)
    at_m, at_k = (lax.axis_index(name) for name in ("m", "k"))
    at_ctx = lax.axis_index(CTX)

    weights = lax.all_to_all(jnp.broadcast_to(out_weight[None], (16,) + out_weight.shape), PLANE, 0, 0)

    cot_same = across(cotangent, lambda h, m: (m, h))
    cot_swap = across(cotangent, lambda h, m: (m, 1 - h))
    cot_pair = in_order(cot_same, cot_swap, at_m)

    sent = [key_branch * value_branch, long_filter * norm_scale, query_branch]
    sent = jnp.concatenate([array.T.reshape(n_ctx, group, rows) for array in sent], 1)
    signals = lax.all_to_all(tie(sent, weights, cot_same, cot_swap), CTX, 0, 0)
    weights = weights.transpose(1, 0, 2).reshape(chans, -1)
    product, query = signals[:, :group], signals[:, 2 * group :]

    cot_pair = tie(cot_pair, signals)
    cot_line = lax.all_to_all(jnp.broadcast_to(cot_pair[None], (4,) + cot_pair.shape), "l", 0, 0)
    cot_cores = in_order(cot_line, other_core(cot_line), at_k)
    cot_full = cot_cores.transpose(2, 3, 1, 0, 4).reshape(2 * rows, 8 * chans)

    spectra = forward_fourier(signals[:, : 2 * group], tab)
    prod_real, prod_imag = halves(spectra[:, :group])
    taps_real, taps_imag = halves(spectra[:, group:])
    conv = inverse_fourier(
        prod_real * taps_real - prod_imag * taps_imag, prod_real * taps_imag + prod_imag * taps_real, tab
    )
    skip = lax.dynamic_slice(skip_weight, (at_ctx * group,), (group,))[None, :, None]
    gate = conv + skip * product
    mixed = (gate * query).reshape(2, 16, group, rows).transpose(1, 0, 2, 3)
    mixed = jnp.broadcast_to(mixed[None], (2,) + mixed.shape).reshape(n_ctx, 2, group, rows)
    mixed = lax.all_to_all(tie(mixed, cot_line), CTX, 0, 0)

    mixed_grad = product_of(weights, cot_full, 1, 1)
    mixed_grad = mixed_grad.reshape(n_ctx, group, 2, rows).transpose(0, 2, 1, 3)
    mixed = tie(mixed, mixed_grad)
    grad = lax.all_to_all(tie(mixed_grad, mixed), CTX, 0, 0)
    grad = grad.reshape(2, 16, 2, group, rows).sum(0).transpose(1, 0, 2, 3).reshape(n_ctx, group, rows)
    pre_grad = grad * query
    mixed = mixed.transpose(0, 2, 1, 3).reshape(chans, 2 * rows)

    weight_part = product_of(mixed, cot_full, 1, 0)
    weight_part = weight_part.reshape(chans, 16, rows).transpose(1, 0, 2)
    weight_part = lax.psum_scatter(weight_part, "y", scatter_dimension=0, tiled=True)
    weight_grad = lax.psum_scatter(weight_part, "x", scatter_dimension=0, tiled=False) * norm_scale

    partial = product_of(mixed, weights, 0, 0)
    partial = partial.reshape(2, rows, 4, 2, chans).transpose(3, 2, 0, 1, 4)
    partial_far = pick(partial, 1 - at_k)
    partial = pick(partial, at_k) + jnp.stack([other_core(partial_far[at]) for at in range(4)])
    partial = lax.all_to_all(tie(partial, grad), "l", 0, 0).sum(0)
    partial = tie(partial, weight_part)
    projected = across(pick(partial, at_m), lambda h, m: (m, h))
    projected = projected + across(pick(partial, 1 - at_m), lambda h, m: (1 - m, h))

    grad_real, grad_imag = halves(forward_fourier(pre_grad, tab))
    lead_real = jnp.concatenate([taps_real, prod_real], 1)
    lead_imag = jnp.concatenate([taps_imag, prod_imag], 1)
    grad_real = jnp.concatenate([grad_real, grad_real], 1)
    grad_imag = jnp.concatenate([grad_imag, grad_imag], 1)
    lagged = inverse_fourier(
        grad_real * lead_real + grad_imag * lead_imag, grad_imag * lead_real - grad_real * lead_imag, tab
    )
    prod_grad = tie(lagged[:, :group] + skip * pre_grad, partial)
    skip_part = jnp.sum(pre_grad * product, axis=(0, 2)) * norm_scale
    skip_row = jnp.broadcast_to(jnp.pad(skip_part, (0, rows - group))[None, None], (n_ctx, group, rows))
    back = [prod_grad, lagged[:, group:] * norm_scale, grad * gate, skip_row]
    back = lax.all_to_all(jnp.concatenate(back, 1), CTX, 0, 0)
    product_grad, filter_grad, query_grad = (
        back[:, at * group : (at + 1) * group].reshape(chans, rows).T for at in range(3)
    )
    skip_grad = back[:, 3 * group, :group].reshape(chans)
    return (
        projected,
        product_grad * value_branch,
        product_grad * key_branch,
        query_grad,
        filter_grad,
        skip_grad,
        weight_grad,
    )


def solution(mesh):
    grid = Mesh(mesh.devices.reshape(SIZES), AXES)
    wide = P(("h", "y", "x"), ("m", "l", "k"))
    tall = P(("m", "l", "k"), ("h", "y", "x"))
    flat = P(("m", "l", "k"))
    return jax.shard_map(
        local,
        mesh=grid,
        in_specs=(wide, wide, wide, wide, flat, tall, wide),
        out_specs=(wide, wide, wide, wide, wide, flat, tall),
        check_vma=False,
    )
```

```python
import math

import jax
import jax.numpy as jnp
import numpy as np
from jax import lax
from jax.experimental import pallas as pl
from jax.experimental.pallas import tpu as pltpu
from jax.sharding import Mesh
from jax.sharding import PartitionSpec as P

AXES = ("h", "y", "x", "m", "l", "k")
SIZES = (2, 4, 4, 2, 4, 2)
CTX = ("h", "y", "x")
PLANE = ("y", "x")
side = 128
exact = lax.Precision.HIGHEST
ANY = pl.BlockSpec(memory_space=pl.ANY)
VMEM = pl.BlockSpec(memory_space=pltpu.VMEM)


def tables(seq_len):
    full = 2 * seq_len
    blocks = full // side
    kept = blocks // 2 + 1
    rows = np.arange(kept)
    first = 2.0 * np.pi * np.outer(rows, np.arange(seq_len // side)) / blocks
    turn = 2.0 * np.pi * np.outer(rows, np.arange(side)) / full
    inner = 2.0 * np.pi * np.outer(np.arange(side), np.arange(side)) / side
    weight = np.where((rows == 0) | (rows == blocks // 2), 1.0, 2.0)[:, None] / full
    cos, sin = np.cos(inner), np.sin(inner)
    as32 = lambda a: jnp.asarray(a.astype(np.float32))
    return dict(
        first=as32(np.concatenate([np.cos(first), -np.sin(first)], 0)),
        turn_cos=as32(np.cos(turn))[:, None, :],
        turn_sin=as32(np.sin(turn))[:, None, :],
        inner=as32(np.block([[cos, -sin], [sin, cos]])),
        outer=as32(np.block([[cos, sin], [-sin, cos]])),
        last=as32(np.concatenate([weight * np.cos(first), -weight * np.sin(first)], 0).T),
        kept=kept,
    )


def forward_fourier(signal, tab):
    both = jnp.einsum("kn,ncm->kcm", tab["first"], signal, precision=exact)
    real, imag = both[: tab["kept"]], both[tab["kept"] :]
    turned = jnp.concatenate(
        [real * tab["turn_cos"] + imag * tab["turn_sin"], imag * tab["turn_cos"] - real * tab["turn_sin"]], 2
    )
    return jnp.einsum("kcm,mj->kcj", turned, tab["inner"], precision=exact)


def inverse_fourier(real, imag, tab):
    back = jnp.einsum("kcm,mj->kcj", jnp.concatenate([real, imag], 2), tab["outer"], precision=exact)
    real, imag = back[..., :side], back[..., side:]
    turned = jnp.concatenate(
        [real * tab["turn_cos"] - imag * tab["turn_sin"], imag * tab["turn_cos"] + real * tab["turn_sin"]], 0
    )
    return jnp.einsum("nk,kcm->ncm", tab["last"], turned, precision=exact)


def halves(spectrum):
    return spectrum[..., :side], spectrum[..., side:]


def split(array):
    high = array.astype(jnp.bfloat16)
    return high, (array - high.astype(jnp.float32)).astype(jnp.bfloat16)


def dot3(left, right, left_dim, right_dim):
    def one(a, b):
        return lax.dot_general(a, b, (((left_dim,), (right_dim,)), ((), ())), preferred_element_type=jnp.float32)

    return one(left[0], right[0]) + (one(left[0], right[1]) + one(left[1], right[0]))


def params(mib=24):
    return pltpu.CompilerParams(vmem_limit_bytes=mib << 20)


def cost(flops=0, size=0):
    return pl.CostEstimate(flops=flops, bytes_accessed=size, transcendentals=0)


def prepare_kernel(scale, group, key, value, taps, query, *refs):
    out = refs[-1]
    arrays = (key[...] * value[...], taps[...] * scale, query[...])
    for at, array in enumerate(arrays):
        out[:, at * group : (at + 1) * group, :] = array.T.reshape(out.shape[0], group, out.shape[2])


def prepare(key, value, taps, query, first, scale, n_ctx):
    rows, chans = key.shape
    group = chans // n_ctx
    return pl.pallas_call(
        lambda *refs: prepare_kernel(scale, group, *refs),
        out_shape=jax.ShapeDtypeStruct((n_ctx, 3 * group, rows), jnp.float32),
        in_specs=[VMEM] * 4 + [ANY] * len(first),
        out_specs=VMEM,
        compiler_params=params(),
        cost_estimate=cost(0, 1 << 20),
    )(key, value, taps, query, *first)


def double_kernel(mixed, *refs):
    out = refs[-1]
    half = mixed.shape[0] // 2
    for to in range(2):
        for at in range(2):
            out[to * half : (to + 1) * half, at] = mixed[at * half : (at + 1) * half]


def double(mixed, first):
    blocks, group, rows = mixed.shape
    return pl.pallas_call(
        double_kernel,
        out_shape=jax.ShapeDtypeStruct((blocks, 2, group, rows), jnp.float32),
        in_specs=[VMEM] + [ANY] * len(first),
        out_specs=VMEM,
        compiler_params=params(),
        cost_estimate=cost(0, 1 << 18),
    )(mixed, *first)


def gradient_kernel(at_k, near_w, far_w, near, far, out, total):
    step = pl.program_id(0)
    rows = near.shape[2]

    def term(weight, cot):
        flat = cot[...].reshape(2 * rows, cot.shape[3])
        return dot3(split(weight[...]), split(flat), 1, 1)

    both = term(near_w, near) + term(far_w, far)

    @pl.when(step == 0)
    def _():
        total[...] = both

    @pl.when(step > 0)
    def _():
        total[...] += both

    @pl.when(step == pl.num_programs(0) - 1)
    def _():
        for at in range(2):
            out[:, at] = total[:, at * rows : (at + 1) * rows].reshape(out.shape[0], out.shape[2], rows)


def gradient(weights, near, far, at_k, n_ctx):
    lines, _, rows, wide = near.shape
    chans = weights.shape[0]
    block = pl.BlockSpec((1, 2, rows, wide), lambda l, k: (l, 0, 0, 0))
    return pl.pallas_call(
        gradient_kernel,
        out_shape=jax.ShapeDtypeStruct((n_ctx, 2, chans // n_ctx, rows), jnp.float32),
        grid_spec=pltpu.PrefetchScalarGridSpec(
            num_scalar_prefetch=1,
            grid=(lines,),
            in_specs=[
                pl.BlockSpec((chans, wide), lambda l, k: (0, 2 * l + k[0])),
                pl.BlockSpec((chans, wide), lambda l, k: (0, 2 * l + 1 - k[0])),
                block,
                block,
            ],
            out_specs=pl.BlockSpec((n_ctx, 2, chans // n_ctx, rows), lambda l, k: (0, 0, 0, 0)),
            scratch_shapes=[pltpu.VMEM((chans, 2 * rows), jnp.float32)],
        ),
        compiler_params=params(),
        cost_estimate=cost(3 * 2 * chans * 2 * rows * 2 * lines * wide, 5 << 20),
    )(at_k, weights, weights, near, far)


def partial_kernel(at_k, mixed, weight, *refs):
    out, high, low = refs[-3:]
    rows = mixed.shape[3]
    chans = weight.shape[0]

    @pl.when(pl.program_id(0) == 0)
    def _():
        for at in range(2):
            turned = split(mixed[:, at].reshape(chans, rows).T)
            high[at * rows : (at + 1) * rows], low[at * rows : (at + 1) * rows] = turned

    value = dot3((high[...], low[...]), split(weight[...]), 1, 0).reshape(out.shape)
    if len(refs) > 3:
        value = value + refs[0][...]
    out[...] = value


def partial_sums(mixed, weights, at_k, far, more=None, first=()):
    chans = weights.shape[0]
    rows = mixed.shape[3]
    lines = weights.shape[1] // (2 * chans)
    flip = 1 if far else 0
    block = pl.BlockSpec((1, 2, rows, chans), lambda l, k: (l, 0, 0, 0))
    return pl.pallas_call(
        partial_kernel,
        out_shape=jax.ShapeDtypeStruct((lines, 2, rows, chans), jnp.float32),
        grid_spec=pltpu.PrefetchScalarGridSpec(
            num_scalar_prefetch=1,
            grid=(lines,),
            in_specs=[
                pl.BlockSpec(mixed.shape, lambda l, k: (0, 0, 0, 0)),
                pl.BlockSpec((chans, chans), lambda l, k: (0, 2 * l + (k[0] + flip) % 2)),
            ]
            + ([block] if more is not None else [])
            + [ANY] * len(first),
            out_specs=block,
            scratch_shapes=[pltpu.VMEM((2 * rows, chans), jnp.bfloat16)] * 2,
        ),
        compiler_params=params(),
        cost_estimate=cost(3 * 2 * chans * 2 * rows * lines * chans, 3 << 20),
    )(at_k, mixed, weights, *([more] if more is not None else []), *first)


def outer_kernel(at_k, mixed, near, far, out, high, low):
    rows = mixed.shape[3]
    chans = out.shape[1]

    @pl.when(pl.program_id(0) == 0)
    def _():
        for at in range(2):
            turned = split(mixed[:, at].reshape(chans, rows))
            high[:, at * rows : (at + 1) * rows], low[:, at * rows : (at + 1) * rows] = turned

    for cot, core in ((near, at_k[0]), (far, 1 - at_k[0])):
        flat = cot[...].reshape(2 * rows, cot.shape[3])
        value = dot3((high[...], low[...]), split(flat), 1, 0)
        for at in range(2):
            out[2 * core + at] = value[:, at * rows : (at + 1) * rows]


def outer(mixed, near, far, at_k):
    lines, _, rows, wide = near.shape
    chans = mixed.shape[0] * mixed.shape[2]
    block = pl.BlockSpec((1, 2, rows, wide), lambda l, k: (l, 0, 0, 0))
    return pl.pallas_call(
        outer_kernel,
        out_shape=jax.ShapeDtypeStruct((4 * lines, chans, rows), jnp.float32),
        grid_spec=pltpu.PrefetchScalarGridSpec(
            num_scalar_prefetch=1,
            grid=(lines,),
            in_specs=[pl.BlockSpec(mixed.shape, lambda l, k: (0, 0, 0, 0)), block, block],
            out_specs=pl.BlockSpec((4, chans, rows), lambda l, k: (l, 0, 0)),
            scratch_shapes=[pltpu.VMEM((chans, 2 * rows), jnp.bfloat16)] * 2,
        ),
        compiler_params=params(),
        cost_estimate=cost(3 * 2 * chans * 2 * rows * 2 * lines * wide, 5 << 20),
    )(at_k, mixed, near, far)


def returned_kernel(scale, group, lagged, pre_grad, signals, grad, gate, skip, *refs):
    out = refs[-1]
    pre = pre_grad[...]
    out[:, :group] = lagged[:, :group] + skip[...][None] * pre
    out[:, group : 2 * group] = lagged[:, group:] * scale
    out[:, 2 * group : 3 * group] = grad[...] * gate[...]
    skip_grad = jnp.sum(jnp.sum(pre * signals[:, :group], axis=0), axis=1, keepdims=True) * scale
    out[:, 3 * group :] = jnp.broadcast_to(skip_grad[None], out.shape[:1] + (group,) + out.shape[2:])


def returned(lagged, pre_grad, signals, grad, gate, skip, first, scale):
    blocks, group, rows = pre_grad.shape
    return pl.pallas_call(
        lambda *refs: returned_kernel(scale, group, *refs),
        out_shape=jax.ShapeDtypeStruct((blocks, 4 * group, rows), jnp.float32),
        in_specs=[VMEM] * 6 + [ANY] * len(first),
        out_specs=VMEM,
        compiler_params=params(),
        cost_estimate=cost(0, 1 << 20),
    )(lagged, pre_grad, signals, grad, gate, skip, *first)


def finish_kernel(group, back, key, value, key_grad, value_grad, query_grad, filter_grad, skip_grad):
    rows, chans = key.shape

    def turned(at):
        return back[:, at * group : (at + 1) * group, :].reshape(chans, rows).T

    product_grad = turned(0)
    key_grad[...] = product_grad * value[...]
    value_grad[...] = product_grad * key[...]
    filter_grad[...] = turned(1)
    query_grad[...] = turned(2)
    skip_grad[...] = turned(3)[:1]


def finish(back, key, value, group):
    whole = jax.ShapeDtypeStruct(key.shape, jnp.float32)
    return pl.pallas_call(
        lambda *refs: finish_kernel(group, *refs),
        out_shape=[whole] * 4 + [jax.ShapeDtypeStruct((1, key.shape[1]), jnp.float32)],
        in_specs=[VMEM] * 3,
        out_specs=[VMEM] * 5,
        compiler_params=params(),
        cost_estimate=cost(0, 1 << 20),
    )(back, key, value)


def across(block, target):
    pairs = []
    for h in range(2):
        for m in range(2):
            to_h, to_m = target(h, m)
            pairs.append((h * 2 + m, to_h * 2 + to_m))
    return lax.ppermute(block, ("h", "m"), pairs)


def other_core(block):
    return lax.ppermute(block, "k", [(0, 1), (1, 0)])


def in_order(own, other, at):
    return jnp.where(at == 0, jnp.stack([own, other]), jnp.stack([other, own]))


def tie(value, *first):
    for array in first:
        value = value + 0.0 * array[(0,) * array.ndim]
    return value


def pick(pair, at):
    return lax.dynamic_index_in_dim(pair, at, 0, False)


def local(key_branch, value_branch, query_branch, long_filter, skip_weight, out_weight, cotangent):
    rows, chans = key_branch.shape
    n_ctx = 32
    group = chans // n_ctx
    seq_len = rows * n_ctx
    norm_scale = 1.0 / math.sqrt(seq_len)
    tab = tables(seq_len)
    at_m = lax.axis_index("m")
    at_k = lax.axis_index("k").astype(jnp.int32).reshape(1)
    at_ctx = lax.axis_index(CTX)

    weights = lax.all_gather(out_weight, PLANE, axis=1, tiled=True)

    cot_same = across(cotangent, lambda h, m: (m, h))
    cot_swap = across(cotangent, lambda h, m: (m, 1 - h))
    cot_pair = in_order(cot_same, cot_swap, at_m)

    sent = prepare(key_branch, value_branch, long_filter, query_branch, (), norm_scale, n_ctx)
    signals = lax.all_to_all(sent, CTX, 0, 0)
    product, query = signals[:, :group], signals[:, 2 * group :]

    cot_pair = tie(cot_pair, signals)
    near = lax.all_to_all(jnp.broadcast_to(cot_pair[None], (4,) + cot_pair.shape), "l", 0, 0)
    far = other_core(near)

    tab["first"] = tie(tab["first"], weights)
    spectra = forward_fourier(signals[:, : 2 * group], tab)
    prod_real, prod_imag = halves(spectra[:, :group])
    taps_real, taps_imag = halves(spectra[:, group:])
    conv = inverse_fourier(
        prod_real * taps_real - prod_imag * taps_imag, prod_real * taps_imag + prod_imag * taps_real, tab
    )
    skip = jnp.broadcast_to(lax.dynamic_slice(skip_weight, (at_ctx * group,), (group,))[:, None], (group, rows))
    gate = conv + skip[None] * product
    mixed = lax.all_to_all(double(gate * query, (near,)), CTX, 0, 0)

    mixed_grad = gradient(weights, near, far, at_k, n_ctx)
    grad_got = lax.all_to_all(mixed_grad + 0.0 * mixed, CTX, 0, 0)
    grad = grad_got.reshape(2, 16, 2, group, rows).sum(0).transpose(1, 0, 2, 3).reshape(n_ctx, group, rows)
    pre_grad = grad * query

    weight_part = outer(mixed, near, far, at_k)
    weight_part = lax.psum_scatter(weight_part, "y", scatter_dimension=0, tiled=True)
    weight_grad = lax.psum_scatter(weight_part, "x", scatter_dimension=0, tiled=False) * norm_scale

    partial_far = partial_sums(mixed, weights, at_k, True)
    partial_far = jnp.concatenate([other_core(partial_far[at : at + 2]) for at in range(0, 4, 2)])
    partial = partial_sums(mixed, weights, at_k, False, partial_far, (grad_got,))
    line_got = lax.all_to_all(partial, "l", 0, 0)
    partial = tie(line_got.sum(0), weight_part)
    projected = across(pick(partial, at_m), lambda h, m: (m, h))
    projected = projected + across(pick(partial, 1 - at_m), lambda h, m: (1 - m, h))

    grad_real, grad_imag = halves(forward_fourier(pre_grad, tab))
    lead_real = jnp.concatenate([taps_real, prod_real], 1)
    lead_imag = jnp.concatenate([taps_imag, prod_imag], 1)
    grad_real = jnp.concatenate([grad_real, grad_real], 1)
    grad_imag = jnp.concatenate([grad_imag, grad_imag], 1)
    lagged = inverse_fourier(
        grad_real * lead_real + grad_imag * lead_imag, grad_imag * lead_real - grad_real * lead_imag, tab
    )
    back = returned(lagged, pre_grad, signals, grad, gate, skip, (line_got,), norm_scale)
    back = lax.all_to_all(back, CTX, 0, 0)
    key_grad, value_grad, query_grad, filter_grad, skip_grad = finish(back, key_branch, value_branch, group)
    return (projected, key_grad, value_grad, query_grad, filter_grad, skip_grad.reshape(chans), weight_grad)


def solution(mesh):
    grid = Mesh(mesh.devices.reshape(SIZES), AXES)
    wide = P(("h", "y", "x"), ("m", "l", "k"))
    tall = P(("m", "l", "k"), ("h", "y", "x"))
    flat = P(("m", "l", "k"))
    return jax.shard_map(
        local,
        mesh=grid,
        in_specs=(wide, wide, wide, wide, flat, tall, wide),
        out_specs=(wide, wide, wide, wide, wide, flat, tall),
        check_vma=False,
    )
```

```python
import math

import jax
import jax.numpy as jnp
import numpy as np
from jax import lax
from jax.experimental import pallas as pl
from jax.experimental.pallas import tpu as pltpu
from jax.sharding import Mesh
from jax.sharding import PartitionSpec as P

AXES = ("h", "y", "x", "m", "l", "k")
SIZES = (2, 4, 4, 2, 4, 2)
CTX = ("h", "y", "x")
PLANE = ("y", "x")
side = 128
exact = lax.Precision.HIGHEST
ANY = pl.BlockSpec(memory_space=pl.ANY)
VMEM = pl.BlockSpec(memory_space=pltpu.VMEM)


def tables(seq_len):
    full = 2 * seq_len
    blocks = full // side
    kept = blocks // 2 + 1
    rows = np.arange(kept)
    first = 2.0 * np.pi * np.outer(rows, np.arange(seq_len // side)) / blocks
    turn = 2.0 * np.pi * np.outer(rows, np.arange(side)) / full
    inner = 2.0 * np.pi * np.outer(np.arange(side), np.arange(side)) / side
    weight = np.where((rows == 0) | (rows == blocks // 2), 1.0, 2.0)[:, None] / full
    cos, sin = np.cos(inner), np.sin(inner)
    as32 = lambda a: jnp.asarray(a.astype(np.float32))
    return dict(
        first=as32(np.concatenate([np.cos(first), -np.sin(first)], 0)),
        turn_cos=as32(np.cos(turn))[:, None, :],
        turn_sin=as32(np.sin(turn))[:, None, :],
        inner=as32(np.block([[cos, -sin], [sin, cos]])),
        outer=as32(np.block([[cos, sin], [-sin, cos]])),
        last=as32(np.concatenate([weight * np.cos(first), -weight * np.sin(first)], 0).T),
        kept=kept,
    )


def forward_fourier(signal, tab):
    both = jnp.einsum("kn,ncm->kcm", tab["first"], signal, precision=exact)
    real, imag = both[: tab["kept"]], both[tab["kept"] :]
    turned = jnp.concatenate(
        [real * tab["turn_cos"] + imag * tab["turn_sin"], imag * tab["turn_cos"] - real * tab["turn_sin"]], 2
    )
    return jnp.einsum("kcm,mj->kcj", turned, tab["inner"], precision=exact)


def inverse_fourier(real, imag, tab):
    back = jnp.einsum("kcm,mj->kcj", jnp.concatenate([real, imag], 2), tab["outer"], precision=exact)
    real, imag = back[..., :side], back[..., side:]
    turned = jnp.concatenate(
        [real * tab["turn_cos"] - imag * tab["turn_sin"], imag * tab["turn_cos"] + real * tab["turn_sin"]], 0
    )
    return jnp.einsum("nk,kcm->ncm", tab["last"], turned, precision=exact)


def halves(spectrum):
    return spectrum[..., :side], spectrum[..., side:]


def split(array):
    high = array.astype(jnp.bfloat16)
    return high, (array - high.astype(jnp.float32)).astype(jnp.bfloat16)


def dot3(left, right, left_dim, right_dim):
    def one(a, b):
        return lax.dot_general(a, b, (((left_dim,), (right_dim,)), ((), ())), preferred_element_type=jnp.float32)

    return one(left[0], right[0]) + (one(left[0], right[1]) + one(left[1], right[0]))


def params(mib=24):
    return pltpu.CompilerParams(vmem_limit_bytes=mib << 20)


def cost(flops=0, size=0):
    return pl.CostEstimate(flops=flops, bytes_accessed=size, transcendentals=0)


def prepare_kernel(scale, group, key, value, taps, query, *refs):
    out = refs[-1]
    arrays = (key[...] * value[...], taps[...] * scale, query[...])
    for at, array in enumerate(arrays):
        out[:, at * group : (at + 1) * group, :] = array.T.reshape(out.shape[0], group, out.shape[2])


def prepare(key, value, taps, query, first, scale, n_ctx):
    rows, chans = key.shape
    group = chans // n_ctx
    return pl.pallas_call(
        lambda *refs: prepare_kernel(scale, group, *refs),
        out_shape=jax.ShapeDtypeStruct((n_ctx, 3 * group, rows), jnp.float32),
        in_specs=[VMEM] * 4 + [ANY] * len(first),
        out_specs=VMEM,
        compiler_params=params(),
        cost_estimate=cost(0, 1 << 20),
    )(key, value, taps, query, *first)


def double_kernel(mixed, *refs):
    out = refs[-1]
    half = mixed.shape[0] // 2
    for to in range(2):
        for at in range(2):
            out[to * half : (to + 1) * half, at] = mixed[at * half : (at + 1) * half]


def double(mixed, first):
    blocks, group, rows = mixed.shape
    return pl.pallas_call(
        double_kernel,
        out_shape=jax.ShapeDtypeStruct((blocks, 2, group, rows), jnp.float32),
        in_specs=[VMEM] + [ANY] * len(first),
        out_specs=VMEM,
        compiler_params=params(),
        cost_estimate=cost(0, 1 << 18),
    )(mixed, *first)


def line_kernel(at_m, same, swap, *refs):
    out = refs[-1]
    for to in range(out.shape[0]):
        out[to, at_m[0]] = same[...]
        out[to, 1 - at_m[0]] = swap[...]


def line_blocks(same, swap, at_m, lines, first):
    return pl.pallas_call(
        line_kernel,
        out_shape=jax.ShapeDtypeStruct((lines, 2) + same.shape, jnp.float32),
        in_specs=[pl.BlockSpec(memory_space=pltpu.SMEM)] + [VMEM] * 2 + [ANY] * len(first),
        out_specs=VMEM,
        compiler_params=params(),
        cost_estimate=cost(0, 1 << 20),
    )(at_m, same, swap, *first)


def pass_kernel(value, *refs):
    refs[-1][...] = value[...]


def after(value, first):
    return pl.pallas_call(
        pass_kernel,
        out_shape=jax.ShapeDtypeStruct(value.shape, jnp.float32),
        in_specs=[VMEM] + [ANY] * len(first),
        out_specs=VMEM,
        compiler_params=params(),
        cost_estimate=cost(0, 1 << 18),
    )(value, *first)


def gradient_kernel(at_k, near_w, far_w, near, far, out, total):
    step = pl.program_id(0)
    rows = near.shape[2]

    def term(weight, cot):
        flat = cot[...].reshape(2 * rows, cot.shape[3])
        return dot3(split(weight[...]), split(flat), 1, 1)

    both = term(near_w, near) + term(far_w, far)

    @pl.when(step == 0)
    def _():
        total[...] = both

    @pl.when(step > 0)
    def _():
        total[...] += both

    @pl.when(step == pl.num_programs(0) - 1)
    def _():
        for at in range(2):
            out[:, at] = total[:, at * rows : (at + 1) * rows].reshape(out.shape[0], out.shape[2], rows)


def gradient(weights, near, far, at_k, n_ctx):
    lines, _, rows, wide = near.shape
    chans = weights.shape[0]
    block = pl.BlockSpec((1, 2, rows, wide), lambda l, k: (l, 0, 0, 0))
    return pl.pallas_call(
        gradient_kernel,
        out_shape=jax.ShapeDtypeStruct((n_ctx, 2, chans // n_ctx, rows), jnp.float32),
        grid_spec=pltpu.PrefetchScalarGridSpec(
            num_scalar_prefetch=1,
            grid=(lines,),
            in_specs=[
                pl.BlockSpec((chans, wide), lambda l, k: (0, 2 * l + k[0])),
                pl.BlockSpec((chans, wide), lambda l, k: (0, 2 * l + 1 - k[0])),
                block,
                block,
            ],
            out_specs=pl.BlockSpec((n_ctx, 2, chans // n_ctx, rows), lambda l, k: (0, 0, 0, 0)),
            scratch_shapes=[pltpu.VMEM((chans, 2 * rows), jnp.float32)],
        ),
        compiler_params=params(),
        cost_estimate=cost(3 * 2 * chans * 2 * rows * 2 * lines * wide, 5 << 20),
    )(at_k, weights, weights, near, far)


def partial_kernel(at_k, mixed, weight, *refs):
    out, high, low = refs[-3:]
    rows = mixed.shape[3]
    chans = weight.shape[0]

    @pl.when(pl.program_id(0) == 0)
    def _():
        for at in range(2):
            turned = split(mixed[:, at].reshape(chans, rows).T)
            high[at * rows : (at + 1) * rows], low[at * rows : (at + 1) * rows] = turned

    value = dot3((high[...], low[...]), split(weight[...]), 1, 0).reshape(out.shape)
    if len(refs) > 3:
        value = value + refs[0][...]
    out[...] = value


def partial_sums(mixed, weights, at_k, far, more=None, first=()):
    chans = weights.shape[0]
    rows = mixed.shape[3]
    lines = weights.shape[1] // (2 * chans)
    flip = 1 if far else 0
    block = pl.BlockSpec((1, 2, rows, chans), lambda l, k: (l, 0, 0, 0))
    return pl.pallas_call(
        partial_kernel,
        out_shape=jax.ShapeDtypeStruct((lines, 2, rows, chans), jnp.float32),
        grid_spec=pltpu.PrefetchScalarGridSpec(
            num_scalar_prefetch=1,
            grid=(lines,),
            in_specs=[
                pl.BlockSpec(mixed.shape, lambda l, k: (0, 0, 0, 0)),
                pl.BlockSpec((chans, chans), lambda l, k: (0, 2 * l + (k[0] + flip) % 2)),
            ]
            + ([block] if more is not None else [])
            + [ANY] * len(first),
            out_specs=block,
            scratch_shapes=[pltpu.VMEM((2 * rows, chans), jnp.bfloat16)] * 2,
        ),
        compiler_params=params(),
        cost_estimate=cost(3 * 2 * chans * 2 * rows * lines * chans, 3 << 20),
    )(at_k, mixed, weights, *([more] if more is not None else []), *first)


def outer_kernel(at_k, mixed, near, far, out, high, low):
    rows = mixed.shape[3]
    chans = out.shape[1]

    @pl.when(pl.program_id(0) == 0)
    def _():
        for at in range(2):
            turned = split(mixed[:, at].reshape(chans, rows))
            high[:, at * rows : (at + 1) * rows], low[:, at * rows : (at + 1) * rows] = turned

    for cot, core in ((near, at_k[0]), (far, 1 - at_k[0])):
        flat = cot[...].reshape(2 * rows, cot.shape[3])
        value = dot3((high[...], low[...]), split(flat), 1, 0)
        for at in range(2):
            out[2 * core + at] = value[:, at * rows : (at + 1) * rows]


def outer(mixed, near, far, at_k):
    lines, _, rows, wide = near.shape
    chans = mixed.shape[0] * mixed.shape[2]
    block = pl.BlockSpec((1, 2, rows, wide), lambda l, k: (l, 0, 0, 0))
    return pl.pallas_call(
        outer_kernel,
        out_shape=jax.ShapeDtypeStruct((4 * lines, chans, rows), jnp.float32),
        grid_spec=pltpu.PrefetchScalarGridSpec(
            num_scalar_prefetch=1,
            grid=(lines,),
            in_specs=[pl.BlockSpec(mixed.shape, lambda l, k: (0, 0, 0, 0)), block, block],
            out_specs=pl.BlockSpec((4, chans, rows), lambda l, k: (l, 0, 0)),
            scratch_shapes=[pltpu.VMEM((chans, 2 * rows), jnp.bfloat16)] * 2,
        ),
        compiler_params=params(),
        cost_estimate=cost(3 * 2 * chans * 2 * rows * 2 * lines * wide, 5 << 20),
    )(at_k, mixed, near, far)


def returned_kernel(scale, group, lagged, pre_grad, signals, grad, gate, skip, *refs):
    out = refs[-1]
    pre = pre_grad[...]
    out[:, :group] = lagged[:, :group] + skip[...][None] * pre
    out[:, group : 2 * group] = lagged[:, group:] * scale
    out[:, 2 * group : 3 * group] = grad[...] * gate[...]
    skip_grad = jnp.sum(jnp.sum(pre * signals[:, :group], axis=0), axis=1, keepdims=True) * scale
    out[:, 3 * group :] = jnp.broadcast_to(skip_grad[None], out.shape[:1] + (group,) + out.shape[2:])


def returned(lagged, pre_grad, signals, grad, gate, skip, first, scale):
    blocks, group, rows = pre_grad.shape
    return pl.pallas_call(
        lambda *refs: returned_kernel(scale, group, *refs),
        out_shape=jax.ShapeDtypeStruct((blocks, 4 * group, rows), jnp.float32),
        in_specs=[VMEM] * 6 + [ANY] * len(first),
        out_specs=VMEM,
        compiler_params=params(),
        cost_estimate=cost(0, 1 << 20),
    )(lagged, pre_grad, signals, grad, gate, skip, *first)


def finish_kernel(group, back, key, value, key_grad, value_grad, query_grad, filter_grad, skip_grad):
    rows, chans = key.shape

    def turned(at):
        return back[:, at * group : (at + 1) * group, :].reshape(chans, rows).T

    product_grad = turned(0)
    key_grad[...] = product_grad * value[...]
    value_grad[...] = product_grad * key[...]
    filter_grad[...] = turned(1)
    query_grad[...] = turned(2)
    skip_grad[...] = turned(3)[:1]


def finish(back, key, value, group):
    whole = jax.ShapeDtypeStruct(key.shape, jnp.float32)
    return pl.pallas_call(
        lambda *refs: finish_kernel(group, *refs),
        out_shape=[whole] * 4 + [jax.ShapeDtypeStruct((1, key.shape[1]), jnp.float32)],
        in_specs=[VMEM] * 3,
        out_specs=[VMEM] * 5,
        compiler_params=params(),
        cost_estimate=cost(0, 1 << 20),
    )(back, key, value)


def across(block, target):
    pairs = []
    for h in range(2):
        for m in range(2):
            to_h, to_m = target(h, m)
            pairs.append((h * 2 + m, to_h * 2 + to_m))
    return lax.ppermute(block, ("h", "m"), pairs)


def other_core(block):
    return lax.ppermute(block, "k", [(0, 1), (1, 0)])


def pick(pair, at):
    return lax.dynamic_index_in_dim(pair, at, 0, False)


def local(key_branch, value_branch, query_branch, long_filter, skip_weight, out_weight, cotangent):
    rows, chans = key_branch.shape
    n_ctx = 32
    group = chans // n_ctx
    seq_len = rows * n_ctx
    norm_scale = 1.0 / math.sqrt(seq_len)
    tab = tables(seq_len)
    at_m, at_k = (lax.axis_index(name).astype(jnp.int32).reshape(1) for name in ("m", "k"))
    at_ctx = lax.axis_index(CTX)

    weights = lax.all_gather(out_weight, PLANE, axis=1, tiled=True)

    cot_same = across(cotangent, lambda h, m: (m, h))
    cot_swap = across(cotangent, lambda h, m: (m, 1 - h))

    sent = prepare(key_branch, value_branch, long_filter, query_branch, (), norm_scale, n_ctx)
    signals = lax.all_to_all(sent, CTX, 0, 0)
    product, query = signals[:, :group], signals[:, 2 * group :]

    spectra = forward_fourier(signals[:, : 2 * group], tab)
    prod_real, prod_imag = halves(spectra[:, :group])
    taps_real, taps_imag = halves(spectra[:, group:])
    conv = inverse_fourier(
        prod_real * taps_real - prod_imag * taps_imag, prod_real * taps_imag + prod_imag * taps_real, tab
    )
    skip = jnp.broadcast_to(lax.dynamic_slice(skip_weight, (at_ctx * group,), (group,))[:, None], (group, rows))
    gate = conv + skip[None] * product
    mixed = lax.all_to_all(double(gate * query, ()), CTX, 0, 0)

    near = line_blocks(cot_same, cot_swap, at_m, 4, (mixed,))
    near = lax.all_to_all(near, "l", 0, 0)
    far = other_core(near)

    partial = partial_sums(mixed, weights, at_k, True)
    partial = jnp.concatenate([other_core(partial[at : at + 2]) for at in range(0, 4, 2)])
    partial = partial_sums(mixed, weights, at_k, False, partial, (near,))
    line_got = lax.all_to_all(partial, "l", 0, 0)
    partial = line_got.sum(0)
    projected = across(pick(partial, at_m[0]), lambda h, m: (m, h))
    projected = projected + across(pick(partial, 1 - at_m[0]), lambda h, m: (1 - m, h))

    weight_part = outer(mixed, near, far, at_k)
    weight_part = lax.psum_scatter(weight_part, "y", scatter_dimension=0, tiled=True)
    weight_grad = lax.psum_scatter(weight_part, "x", scatter_dimension=0, tiled=False) * norm_scale

    mixed_grad = gradient(weights, near, far, at_k, n_ctx)
    grad_got = lax.all_to_all(after(mixed_grad, (line_got,)), CTX, 0, 0)
    grad = grad_got.reshape(2, 16, 2, group, rows).sum(0).transpose(1, 0, 2, 3).reshape(n_ctx, group, rows)
    pre_grad = grad * query

    grad_real, grad_imag = halves(forward_fourier(pre_grad, tab))
    lead_real = jnp.concatenate([taps_real, prod_real], 1)
    lead_imag = jnp.concatenate([taps_imag, prod_imag], 1)
    grad_real = jnp.concatenate([grad_real, grad_real], 1)
    grad_imag = jnp.concatenate([grad_imag, grad_imag], 1)
    lagged = inverse_fourier(
        grad_real * lead_real + grad_imag * lead_imag, grad_imag * lead_real - grad_real * lead_imag, tab
    )
    back = returned(lagged, pre_grad, signals, grad, gate, skip, (projected, weight_part), norm_scale)
    back = lax.all_to_all(back, CTX, 0, 0)
    key_grad, value_grad, query_grad, filter_grad, skip_grad = finish(back, key_branch, value_branch, group)
    return (projected, key_grad, value_grad, query_grad, filter_grad, skip_grad.reshape(chans), weight_grad)


def solution(mesh):
    grid = Mesh(mesh.devices.reshape(SIZES), AXES)
    wide = P(("h", "y", "x"), ("m", "l", "k"))
    tall = P(("m", "l", "k"), ("h", "y", "x"))
    flat = P(("m", "l", "k"))
    return jax.shard_map(
        local,
        mesh=grid,
        in_specs=(wide, wide, wide, wide, flat, tall, wide),
        out_specs=(wide, wide, wide, wide, wide, flat, tall),
        check_vma=False,
    )
```

```python
import math

import jax
import jax.numpy as jnp
import numpy as np
from jax import lax
from jax.experimental import pallas as pl
from jax.experimental.pallas import tpu as pltpu
from jax.sharding import Mesh
from jax.sharding import PartitionSpec as P

AXES = ("h", "y", "x", "m", "l", "k")
SIZES = (2, 4, 4, 2, 4, 2)
CTX = ("h", "y", "x")
PLANE = ("y", "x")
side = 128
exact = lax.Precision.HIGHEST
ANY = pl.BlockSpec(memory_space=pl.ANY)
VMEM = pl.BlockSpec(memory_space=pltpu.VMEM)


def tables(seq_len):
    full = 2 * seq_len
    blocks = full // side
    kept = blocks // 2 + 1
    rows = np.arange(kept)
    first = 2.0 * np.pi * np.outer(rows, np.arange(seq_len // side)) / blocks
    turn = 2.0 * np.pi * np.outer(rows, np.arange(side)) / full
    inner = 2.0 * np.pi * np.outer(np.arange(side), np.arange(side)) / side
    weight = np.where((rows == 0) | (rows == blocks // 2), 1.0, 2.0)[:, None] / full
    cos, sin = np.cos(inner), np.sin(inner)
    as32 = lambda a: jnp.asarray(a.astype(np.float32))
    return dict(
        first=as32(np.concatenate([np.cos(first), -np.sin(first)], 0)),
        turn_cos=as32(np.cos(turn))[:, None, :],
        turn_sin=as32(np.sin(turn))[:, None, :],
        inner=as32(np.block([[cos, -sin], [sin, cos]])),
        outer=as32(np.block([[cos, sin], [-sin, cos]])),
        last=as32(np.concatenate([weight * np.cos(first), -weight * np.sin(first)], 0).T),
        kept=kept,
    )


def forward_fourier(signal, tab):
    both = jnp.einsum("kn,ncm->kcm", tab["first"], signal, precision=exact)
    real, imag = both[: tab["kept"]], both[tab["kept"] :]
    turned = jnp.concatenate(
        [real * tab["turn_cos"] + imag * tab["turn_sin"], imag * tab["turn_cos"] - real * tab["turn_sin"]], 2
    )
    return jnp.einsum("kcm,mj->kcj", turned, tab["inner"], precision=exact)


def inverse_fourier(real, imag, tab):
    back = jnp.einsum("kcm,mj->kcj", jnp.concatenate([real, imag], 2), tab["outer"], precision=exact)
    real, imag = back[..., :side], back[..., side:]
    turned = jnp.concatenate(
        [real * tab["turn_cos"] - imag * tab["turn_sin"], imag * tab["turn_cos"] + real * tab["turn_sin"]], 0
    )
    return jnp.einsum("nk,kcm->ncm", tab["last"], turned, precision=exact)


def halves(spectrum):
    return spectrum[..., :side], spectrum[..., side:]


def split(array):
    high = array.astype(jnp.bfloat16)
    return high, (array - high.astype(jnp.float32)).astype(jnp.bfloat16)


def dot3(left, right, left_dim, right_dim):
    def one(a, b):
        return lax.dot_general(a, b, (((left_dim,), (right_dim,)), ((), ())), preferred_element_type=jnp.float32)

    return one(left[0], right[0]) + (one(left[0], right[1]) + one(left[1], right[0]))


def params(mib=24):
    return pltpu.CompilerParams(vmem_limit_bytes=mib << 20)


def cost(flops=0, size=0):
    return pl.CostEstimate(flops=flops, bytes_accessed=size, transcendentals=0)


def prepare_kernel(scale, group, key, value, taps, query, *refs):
    out = refs[-1]
    arrays = (key[...] * value[...], taps[...] * scale, query[...])
    for at, array in enumerate(arrays):
        out[:, at * group : (at + 1) * group, :] = array.T.reshape(out.shape[0], group, out.shape[2])


def prepare(key, value, taps, query, first, scale, n_ctx):
    rows, chans = key.shape
    group = chans // n_ctx
    return pl.pallas_call(
        lambda *refs: prepare_kernel(scale, group, *refs),
        out_shape=jax.ShapeDtypeStruct((n_ctx, 3 * group, rows), jnp.float32),
        in_specs=[VMEM] * 4 + [ANY] * len(first),
        out_specs=VMEM,
        compiler_params=params(),
        cost_estimate=cost(0, 1 << 20),
    )(key, value, taps, query, *first)


def double_kernel(mixed, *refs):
    out = refs[-1]
    half = mixed.shape[0] // 2
    for to in range(2):
        for at in range(2):
            out[to * half : (to + 1) * half, at] = mixed[at * half : (at + 1) * half]


def double(mixed, first):
    blocks, group, rows = mixed.shape
    return pl.pallas_call(
        double_kernel,
        out_shape=jax.ShapeDtypeStruct((blocks, 2, group, rows), jnp.float32),
        in_specs=[VMEM] + [ANY] * len(first),
        out_specs=VMEM,
        compiler_params=params(),
        cost_estimate=cost(0, 1 << 18),
    )(mixed, *first)


def line_kernel(at_m, same, swap, *refs):
    out = refs[-1]
    for to in range(out.shape[0]):
        out[to, at_m[0]] = same[...]
        out[to, 1 - at_m[0]] = swap[...]


def line_blocks(same, swap, at_m, lines, first):
    return pl.pallas_call(
        line_kernel,
        out_shape=jax.ShapeDtypeStruct((lines, 2) + same.shape, jnp.float32),
        in_specs=[pl.BlockSpec(memory_space=pltpu.SMEM)] + [VMEM] * 2 + [ANY] * len(first),
        out_specs=VMEM,
        compiler_params=params(),
        cost_estimate=cost(0, 1 << 20),
    )(at_m, same, swap, *first)


def pass_kernel(value, *refs):
    refs[-1][...] = value[...]


def after(value, first):
    return pl.pallas_call(
        pass_kernel,
        out_shape=jax.ShapeDtypeStruct(value.shape, jnp.float32),
        in_specs=[VMEM] + [ANY] * len(first),
        out_specs=VMEM,
        compiler_params=params(),
        cost_estimate=cost(0, 1 << 18),
    )(value, *first)


def gradient_kernel(at_k, near_w, far_w, near, far, out, total):
    step = pl.program_id(0)
    rows = near.shape[2]

    def term(weight, cot):
        flat = cot[...].reshape(2 * rows, cot.shape[3])
        return dot3(split(weight[...]), split(flat), 1, 1)

    both = term(near_w, near) + term(far_w, far)

    @pl.when(step == 0)
    def _():
        total[...] = both

    @pl.when(step > 0)
    def _():
        total[...] += both

    @pl.when(step == pl.num_programs(0) - 1)
    def _():
        for at in range(2):
            out[:, at] = total[:, at * rows : (at + 1) * rows].reshape(out.shape[0], out.shape[2], rows)


def gradient(weights, near, far, at_k, n_ctx):
    lines, _, rows, wide = near.shape
    chans = weights.shape[0]
    block = pl.BlockSpec((1, 2, rows, wide), lambda l, k: (l, 0, 0, 0))
    return pl.pallas_call(
        gradient_kernel,
        out_shape=jax.ShapeDtypeStruct((n_ctx, 2, chans // n_ctx, rows), jnp.float32),
        grid_spec=pltpu.PrefetchScalarGridSpec(
            num_scalar_prefetch=1,
            grid=(lines,),
            in_specs=[
                pl.BlockSpec((chans, wide), lambda l, k: (0, 2 * l + k[0])),
                pl.BlockSpec((chans, wide), lambda l, k: (0, 2 * l + 1 - k[0])),
                block,
                block,
            ],
            out_specs=pl.BlockSpec((n_ctx, 2, chans // n_ctx, rows), lambda l, k: (0, 0, 0, 0)),
            scratch_shapes=[pltpu.VMEM((chans, 2 * rows), jnp.float32)],
        ),
        compiler_params=params(),
        cost_estimate=cost(3 * 2 * chans * 2 * rows * 2 * lines * wide, 5 << 20),
    )(at_k, weights, weights, near, far)


def partial_kernel(at_k, mixed, weight, *refs):
    out, high, low = refs[-3:]
    rows = mixed.shape[3]
    chans = weight.shape[0]

    @pl.when(pl.program_id(0) == 0)
    def _():
        for at in range(2):
            turned = split(mixed[:, at].reshape(chans, rows).T)
            high[at * rows : (at + 1) * rows], low[at * rows : (at + 1) * rows] = turned

    value = dot3((high[...], low[...]), split(weight[...]), 1, 0).reshape(out.shape)
    if len(refs) > 3:
        value = value + refs[0][...]
    out[...] = value


def partial_sums(mixed, weights, at_k, far, more=None, first=()):
    chans = weights.shape[0]
    rows = mixed.shape[3]
    lines = weights.shape[1] // (2 * chans)
    flip = 1 if far else 0
    block = pl.BlockSpec((1, 2, rows, chans), lambda l, k: (l, 0, 0, 0))
    return pl.pallas_call(
        partial_kernel,
        out_shape=jax.ShapeDtypeStruct((lines, 2, rows, chans), jnp.float32),
        grid_spec=pltpu.PrefetchScalarGridSpec(
            num_scalar_prefetch=1,
            grid=(lines,),
            in_specs=[
                pl.BlockSpec(mixed.shape, lambda l, k: (0, 0, 0, 0)),
                pl.BlockSpec((chans, chans), lambda l, k: (0, 2 * l + (k[0] + flip) % 2)),
            ]
            + ([block] if more is not None else [])
            + [ANY] * len(first),
            out_specs=block,
            scratch_shapes=[pltpu.VMEM((2 * rows, chans), jnp.bfloat16)] * 2,
        ),
        compiler_params=params(),
        cost_estimate=cost(3 * 2 * chans * 2 * rows * lines * chans, 3 << 20),
    )(at_k, mixed, weights, *([more] if more is not None else []), *first)


def outer_kernel(at_k, mixed, near, far, out, high, low):
    rows = mixed.shape[3]
    chans = out.shape[1]

    @pl.when(pl.program_id(0) == 0)
    def _():
        for at in range(2):
            turned = split(mixed[:, at].reshape(chans, rows))
            high[:, at * rows : (at + 1) * rows], low[:, at * rows : (at + 1) * rows] = turned

    for cot, core in ((near, at_k[0]), (far, 1 - at_k[0])):
        flat = cot[...].reshape(2 * rows, cot.shape[3])
        value = dot3((high[...], low[...]), split(flat), 1, 0)
        for at in range(2):
            out[2 * core + at] = value[:, at * rows : (at + 1) * rows]


def outer(mixed, near, far, at_k):
    lines, _, rows, wide = near.shape
    chans = mixed.shape[0] * mixed.shape[2]
    block = pl.BlockSpec((1, 2, rows, wide), lambda l, k: (l, 0, 0, 0))
    return pl.pallas_call(
        outer_kernel,
        out_shape=jax.ShapeDtypeStruct((4 * lines, chans, rows), jnp.float32),
        grid_spec=pltpu.PrefetchScalarGridSpec(
            num_scalar_prefetch=1,
            grid=(lines,),
            in_specs=[pl.BlockSpec(mixed.shape, lambda l, k: (0, 0, 0, 0)), block, block],
            out_specs=pl.BlockSpec((4, chans, rows), lambda l, k: (l, 0, 0)),
            scratch_shapes=[pltpu.VMEM((chans, 2 * rows), jnp.bfloat16)] * 2,
        ),
        compiler_params=params(),
        cost_estimate=cost(3 * 2 * chans * 2 * rows * 2 * lines * wide, 5 << 20),
    )(at_k, mixed, near, far)


def returned_kernel(scale, group, lagged, pre_grad, signals, grad, gate, skip, *refs):
    out = refs[-1]
    pre = pre_grad[...]
    out[:, :group] = lagged[:, :group] + skip[...][None] * pre
    out[:, group : 2 * group] = lagged[:, group:] * scale
    out[:, 2 * group : 3 * group] = grad[...] * gate[...]
    skip_grad = jnp.sum(jnp.sum(pre * signals[:, :group], axis=0), axis=1, keepdims=True) * scale
    out[:, 3 * group :] = jnp.broadcast_to(skip_grad[None], out.shape[:1] + (group,) + out.shape[2:])


def returned(lagged, pre_grad, signals, grad, gate, skip, first, scale):
    blocks, group, rows = pre_grad.shape
    return pl.pallas_call(
        lambda *refs: returned_kernel(scale, group, *refs),
        out_shape=jax.ShapeDtypeStruct((blocks, 4 * group, rows), jnp.float32),
        in_specs=[VMEM] * 6 + [ANY] * len(first),
        out_specs=VMEM,
        compiler_params=params(),
        cost_estimate=cost(0, 1 << 20),
    )(lagged, pre_grad, signals, grad, gate, skip, *first)


def finish_kernel(group, back, key, value, key_grad, value_grad, query_grad, filter_grad, skip_grad):
    rows, chans = key.shape

    def turned(at):
        return back[:, at * group : (at + 1) * group, :].reshape(chans, rows).T

    product_grad = turned(0)
    key_grad[...] = product_grad * value[...]
    value_grad[...] = product_grad * key[...]
    filter_grad[...] = turned(1)
    query_grad[...] = turned(2)
    skip_grad[...] = turned(3)[:1]


def finish(back, key, value, group):
    whole = jax.ShapeDtypeStruct(key.shape, jnp.float32)
    return pl.pallas_call(
        lambda *refs: finish_kernel(group, *refs),
        out_shape=[whole] * 4 + [jax.ShapeDtypeStruct((1, key.shape[1]), jnp.float32)],
        in_specs=[VMEM] * 3,
        out_specs=[VMEM] * 5,
        compiler_params=params(),
        cost_estimate=cost(0, 1 << 20),
    )(back, key, value)


def swap_hm(block):
    return lax.ppermute(block, ("h", "m"), [(h * 2 + m, m * 2 + h) for h in range(2) for m in range(2)])


def other_core(block):
    return lax.ppermute(block, "k", [(0, 1), (1, 0)])


def fold(pair, at, axis, apart):
    pairs = [(here, here ^ apart) for here in range(lax.axis_size(axis))]
    return pick(pair, at) + lax.ppermute(pick(pair, 1 - at), axis, pairs)


def pick(pair, at):
    return lax.dynamic_index_in_dim(pair, at, 0, False)


def local(key_branch, value_branch, query_branch, long_filter, skip_weight, out_weight, cotangent):
    rows, chans = key_branch.shape
    n_ctx = 32
    group = chans // n_ctx
    seq_len = rows * n_ctx
    norm_scale = 1.0 / math.sqrt(seq_len)
    tab = tables(seq_len)
    at_m, at_k = (lax.axis_index(name).astype(jnp.int32).reshape(1) for name in ("m", "k"))
    at_x = lax.axis_index("x")
    at_ctx = lax.axis_index(CTX)

    weights = lax.all_gather(out_weight, PLANE, axis=1, tiled=True)

    cot_same = swap_hm(cotangent)
    cot_swap = lax.ppermute(cot_same, "m", [(0, 1), (1, 0)])

    sent = prepare(key_branch, value_branch, long_filter, query_branch, (), norm_scale, n_ctx)
    signals = lax.all_to_all(sent, CTX, 0, 0)
    product, query = signals[:, :group], signals[:, 2 * group :]

    spectra = forward_fourier(signals[:, : 2 * group], tab)
    prod_real, prod_imag = halves(spectra[:, :group])
    taps_real, taps_imag = halves(spectra[:, group:])
    conv = inverse_fourier(
        prod_real * taps_real - prod_imag * taps_imag, prod_real * taps_imag + prod_imag * taps_real, tab
    )
    skip = jnp.broadcast_to(lax.dynamic_slice(skip_weight, (at_ctx * group,), (group,))[:, None], (group, rows))
    gate = conv + skip[None] * product
    mixed = lax.all_to_all(double(gate * query, ()), CTX, 0, 0)

    near = line_blocks(cot_same, cot_swap, at_m, 4, (mixed,))
    near = lax.all_to_all(near, "l", 0, 0)
    far = other_core(near)

    partial = partial_sums(mixed, weights, at_k, True)
    partial = jnp.concatenate([other_core(partial[at : at + 2]) for at in range(0, 4, 2)])
    partial = partial_sums(mixed, weights, at_k, False, partial, (near,))
    line_got = lax.all_to_all(partial, "l", 0, 0)
    partial = line_got.sum(0)
    projected = fold(partial, at_m[0], "m", 1)
    projected = swap_hm(projected)

    weight_part = outer(mixed, near, far, at_k)
    weight_part = lax.psum_scatter(weight_part, "y", scatter_dimension=0, tiled=True)
    weight_grad = fold(weight_part.reshape((2, 2) + weight_part.shape[1:]), at_x // 2, "x", 2)
    weight_grad = fold(weight_grad, at_x % 2, "x", 1) * norm_scale

    mixed_grad = gradient(weights, near, far, at_k, n_ctx)
    grad_got = lax.all_to_all(after(mixed_grad, (line_got,)), CTX, 0, 0)
    grad = grad_got.reshape(2, 16, 2, group, rows).sum(0).transpose(1, 0, 2, 3).reshape(n_ctx, group, rows)
    pre_grad = grad * query

    grad_real, grad_imag = halves(forward_fourier(pre_grad, tab))
    lead_real = jnp.concatenate([taps_real, prod_real], 1)
    lead_imag = jnp.concatenate([taps_imag, prod_imag], 1)
    grad_real = jnp.concatenate([grad_real, grad_real], 1)
    grad_imag = jnp.concatenate([grad_imag, grad_imag], 1)
    lagged = inverse_fourier(
        grad_real * lead_real + grad_imag * lead_imag, grad_imag * lead_real - grad_real * lead_imag, tab
    )
    back = returned(lagged, pre_grad, signals, grad, gate, skip, (projected, weight_part), norm_scale)
    back = lax.all_to_all(back, CTX, 0, 0)
    key_grad, value_grad, query_grad, filter_grad, skip_grad = finish(back, key_branch, value_branch, group)
    return (projected, key_grad, value_grad, query_grad, filter_grad, skip_grad.reshape(chans), weight_grad)


def solution(mesh):
    grid = Mesh(mesh.devices.reshape(SIZES), AXES)
    wide = P(("h", "y", "x"), ("m", "l", "k"))
    tall = P(("m", "l", "k"), ("h", "y", "x"))
    flat = P(("m", "l", "k"))
    return jax.shard_map(
        local,
        mesh=grid,
        in_specs=(wide, wide, wide, wide, flat, tall, wide),
        out_specs=(wide, wide, wide, wide, wide, flat, tall),
        check_vma=False,
    )
```

```python
import math

import jax
import jax.numpy as jnp
import numpy as np
from jax import lax
from jax.experimental import pallas as pl
from jax.experimental.pallas import tpu as pltpu
from jax.sharding import Mesh
from jax.sharding import PartitionSpec as P

AXES = ("h", "y", "x", "m", "l", "k")
SIZES = (2, 4, 4, 2, 4, 2)
CTX = ("h", "y", "x")
PLANE = ("y", "x")
side = 128
exact = lax.Precision.HIGHEST
ANY = pl.BlockSpec(memory_space=pl.ANY)
VMEM = pl.BlockSpec(memory_space=pltpu.VMEM)


def tables(seq_len):
    full = 2 * seq_len
    blocks = full // side
    kept = blocks // 2 + 1
    rows = np.arange(kept)
    first = 2.0 * np.pi * np.outer(rows, np.arange(seq_len // side)) / blocks
    turn = 2.0 * np.pi * np.outer(rows, np.arange(side)) / full
    inner = 2.0 * np.pi * np.outer(np.arange(side), np.arange(side)) / side
    weight = np.where((rows == 0) | (rows == blocks // 2), 1.0, 2.0)[:, None] / full
    cos, sin = np.cos(inner), np.sin(inner)
    as32 = lambda a: jnp.asarray(a.astype(np.float32))
    return dict(
        first=as32(np.concatenate([np.cos(first), -np.sin(first)], 0)),
        turn_cos=as32(np.cos(turn))[:, None, :],
        turn_sin=as32(np.sin(turn))[:, None, :],
        inner=as32(np.block([[cos, -sin], [sin, cos]])),
        outer=as32(np.block([[cos, sin], [-sin, cos]])),
        last=as32(np.concatenate([weight * np.cos(first), -weight * np.sin(first)], 0).T),
        kept=kept,
    )


def forward_fourier(signal, tab):
    both = jnp.einsum("kn,ncm->kcm", tab["first"], signal, precision=exact)
    real, imag = both[: tab["kept"]], both[tab["kept"] :]
    turned = jnp.concatenate(
        [real * tab["turn_cos"] + imag * tab["turn_sin"], imag * tab["turn_cos"] - real * tab["turn_sin"]], 2
    )
    return jnp.einsum("kcm,mj->kcj", turned, tab["inner"], precision=exact)


def inverse_fourier(real, imag, tab):
    back = jnp.einsum("kcm,mj->kcj", jnp.concatenate([real, imag], 2), tab["outer"], precision=exact)
    real, imag = back[..., :side], back[..., side:]
    turned = jnp.concatenate(
        [real * tab["turn_cos"] - imag * tab["turn_sin"], imag * tab["turn_cos"] + real * tab["turn_sin"]], 0
    )
    return jnp.einsum("nk,kcm->ncm", tab["last"], turned, precision=exact)


def halves(spectrum):
    return spectrum[..., :side], spectrum[..., side:]


def split(array):
    high = array.astype(jnp.bfloat16)
    return high, (array - high.astype(jnp.float32)).astype(jnp.bfloat16)


def dot3(left, right, left_dim, right_dim):
    def one(a, b):
        return lax.dot_general(a, b, (((left_dim,), (right_dim,)), ((), ())), preferred_element_type=jnp.float32)

    return one(left[0], right[0]) + (one(left[0], right[1]) + one(left[1], right[0]))


def params(mib=24):
    return pltpu.CompilerParams(vmem_limit_bytes=mib << 20)


def cost(flops=0, size=0):
    return pl.CostEstimate(flops=flops, bytes_accessed=size, transcendentals=0)


def prepare_kernel(scale, group, key, value, taps, query, *refs):
    out = refs[-1]
    arrays = (key[...] * value[...], taps[...] * scale, query[...])
    for at, array in enumerate(arrays):
        out[:, at * group : (at + 1) * group, :] = array.T.reshape(out.shape[0], group, out.shape[2])


def prepare(key, value, taps, query, first, scale, n_ctx):
    rows, chans = key.shape
    group = chans // n_ctx
    return pl.pallas_call(
        lambda *refs: prepare_kernel(scale, group, *refs),
        out_shape=jax.ShapeDtypeStruct((n_ctx, 3 * group, rows), jnp.float32),
        in_specs=[VMEM] * 4 + [ANY] * len(first),
        out_specs=VMEM,
        compiler_params=params(),
        cost_estimate=cost(0, 1 << 20),
    )(key, value, taps, query, *first)


def double_kernel(mixed, *refs):
    out = refs[-1]
    half = mixed.shape[0] // 2
    for to in range(2):
        for at in range(2):
            out[to * half : (to + 1) * half, at] = mixed[at * half : (at + 1) * half]


def double(mixed, first):
    blocks, group, rows = mixed.shape
    return pl.pallas_call(
        double_kernel,
        out_shape=jax.ShapeDtypeStruct((blocks, 2, group, rows), jnp.float32),
        in_specs=[VMEM] + [ANY] * len(first),
        out_specs=VMEM,
        compiler_params=params(),
        cost_estimate=cost(0, 1 << 18),
    )(mixed, *first)


def line_kernel(at_m, same, swap, *refs):
    out = refs[-1]
    for to in range(out.shape[0]):
        out[to, at_m[0]] = same[...]
        out[to, 1 - at_m[0]] = swap[...]


def line_blocks(same, swap, at_m, lines, first):
    return pl.pallas_call(
        line_kernel,
        out_shape=jax.ShapeDtypeStruct((lines, 2) + same.shape, jnp.float32),
        in_specs=[pl.BlockSpec(memory_space=pltpu.SMEM)] + [VMEM] * 2 + [ANY] * len(first),
        out_specs=VMEM,
        compiler_params=params(),
        cost_estimate=cost(0, 1 << 20),
    )(at_m, same, swap, *first)


def pass_kernel(value, *refs):
    refs[-1][...] = value[...]


def after(value, first):
    return pl.pallas_call(
        pass_kernel,
        out_shape=jax.ShapeDtypeStruct(value.shape, jnp.float32),
        in_specs=[VMEM] + [ANY] * len(first),
        out_specs=VMEM,
        compiler_params=params(),
        cost_estimate=cost(0, 1 << 18),
    )(value, *first)


def gradient_kernel(at_k, near_w, far_w, near, far, out, total):
    step = pl.program_id(0)
    rows = near.shape[2]

    def term(weight, cot):
        flat = cot[...].reshape(2 * rows, cot.shape[3])
        return dot3(split(weight[...]), split(flat), 1, 1)

    both = term(near_w, near) + term(far_w, far)

    @pl.when(step == 0)
    def _():
        total[...] = both

    @pl.when(step > 0)
    def _():
        total[...] += both

    @pl.when(step == pl.num_programs(0) - 1)
    def _():
        for at in range(2):
            out[:, at] = total[:, at * rows : (at + 1) * rows].reshape(out.shape[0], out.shape[2], rows)


def gradient(weights, near, far, at_k, n_ctx):
    lines, _, rows, wide = near.shape
    chans = weights.shape[0]
    block = pl.BlockSpec((1, 2, rows, wide), lambda l, k: (l, 0, 0, 0))
    return pl.pallas_call(
        gradient_kernel,
        out_shape=jax.ShapeDtypeStruct((n_ctx, 2, chans // n_ctx, rows), jnp.float32),
        grid_spec=pltpu.PrefetchScalarGridSpec(
            num_scalar_prefetch=1,
            grid=(lines,),
            in_specs=[
                pl.BlockSpec((chans, wide), lambda l, k: (0, 2 * l + k[0])),
                pl.BlockSpec((chans, wide), lambda l, k: (0, 2 * l + 1 - k[0])),
                block,
                block,
            ],
            out_specs=pl.BlockSpec((n_ctx, 2, chans // n_ctx, rows), lambda l, k: (0, 0, 0, 0)),
            scratch_shapes=[pltpu.VMEM((chans, 2 * rows), jnp.float32)],
        ),
        compiler_params=params(),
        cost_estimate=cost(3 * 2 * chans * 2 * rows * 2 * lines * wide, 5 << 20),
    )(at_k, weights, weights, near, far)


def partial_kernel(at_k, mixed, weight, *refs):
    out, high, low = refs[-3:]
    rows = mixed.shape[3]
    chans = weight.shape[0]

    @pl.when(pl.program_id(0) == 0)
    def _():
        for at in range(2):
            turned = split(mixed[:, at].reshape(chans, rows).T)
            high[at * rows : (at + 1) * rows], low[at * rows : (at + 1) * rows] = turned

    value = dot3((high[...], low[...]), split(weight[...]), 1, 0).reshape(out.shape)
    if len(refs) > 3:
        value = value + refs[0][...]
    out[...] = value


def partial_sums(mixed, weights, at_k, far, more=None, first=()):
    chans = weights.shape[0]
    rows = mixed.shape[3]
    lines = weights.shape[1] // (2 * chans)
    flip = 1 if far else 0
    block = pl.BlockSpec((1, 2, rows, chans), lambda l, k: (l, 0, 0, 0))
    return pl.pallas_call(
        partial_kernel,
        out_shape=jax.ShapeDtypeStruct((lines, 2, rows, chans), jnp.float32),
        grid_spec=pltpu.PrefetchScalarGridSpec(
            num_scalar_prefetch=1,
            grid=(lines,),
            in_specs=[
                pl.BlockSpec(mixed.shape, lambda l, k: (0, 0, 0, 0)),
                pl.BlockSpec((chans, chans), lambda l, k: (0, 2 * l + (k[0] + flip) % 2)),
            ]
            + ([block] if more is not None else [])
            + [ANY] * len(first),
            out_specs=block,
            scratch_shapes=[pltpu.VMEM((2 * rows, chans), jnp.bfloat16)] * 2,
        ),
        compiler_params=params(),
        cost_estimate=cost(3 * 2 * chans * 2 * rows * lines * chans, 3 << 20),
    )(at_k, mixed, weights, *([more] if more is not None else []), *first)


def outer_kernel(at_k, mixed, near, far, out, high, low):
    rows = mixed.shape[3]
    chans = out.shape[1]

    @pl.when(pl.program_id(0) == 0)
    def _():
        for at in range(2):
            turned = split(mixed[:, at].reshape(chans, rows))
            high[:, at * rows : (at + 1) * rows], low[:, at * rows : (at + 1) * rows] = turned

    for cot, core in ((near, at_k[0]), (far, 1 - at_k[0])):
        flat = cot[...].reshape(2 * rows, cot.shape[3])
        value = dot3((high[...], low[...]), split(flat), 1, 0)
        for at in range(2):
            out[2 * core + at] = value[:, at * rows : (at + 1) * rows]


def outer(mixed, near, far, at_k):
    lines, _, rows, wide = near.shape
    chans = mixed.shape[0] * mixed.shape[2]
    block = pl.BlockSpec((1, 2, rows, wide), lambda l, k: (l, 0, 0, 0))
    return pl.pallas_call(
        outer_kernel,
        out_shape=jax.ShapeDtypeStruct((4 * lines, chans, rows), jnp.float32),
        grid_spec=pltpu.PrefetchScalarGridSpec(
            num_scalar_prefetch=1,
            grid=(lines,),
            in_specs=[pl.BlockSpec(mixed.shape, lambda l, k: (0, 0, 0, 0)), block, block],
            out_specs=pl.BlockSpec((4, chans, rows), lambda l, k: (l, 0, 0)),
            scratch_shapes=[pltpu.VMEM((chans, 2 * rows), jnp.bfloat16)] * 2,
        ),
        compiler_params=params(),
        cost_estimate=cost(3 * 2 * chans * 2 * rows * 2 * lines * wide, 5 << 20),
    )(at_k, mixed, near, far)


def returned_kernel(scale, group, lagged, pre_grad, signals, grad, gate, skip, *refs):
    out = refs[-1]
    pre = pre_grad[...]
    out[:, :group] = lagged[:, :group] + skip[...][None] * pre
    out[:, group : 2 * group] = lagged[:, group:] * scale
    out[:, 2 * group : 3 * group] = grad[...] * gate[...]
    skip_grad = jnp.sum(jnp.sum(pre * signals[:, :group], axis=0), axis=1, keepdims=True) * scale
    out[:, 3 * group :] = jnp.broadcast_to(skip_grad[None], out.shape[:1] + (group,) + out.shape[2:])


def returned(lagged, pre_grad, signals, grad, gate, skip, first, scale):
    blocks, group, rows = pre_grad.shape
    return pl.pallas_call(
        lambda *refs: returned_kernel(scale, group, *refs),
        out_shape=jax.ShapeDtypeStruct((blocks, 4 * group, rows), jnp.float32),
        in_specs=[VMEM] * 6 + [ANY] * len(first),
        out_specs=VMEM,
        compiler_params=params(),
        cost_estimate=cost(0, 1 << 20),
    )(lagged, pre_grad, signals, grad, gate, skip, *first)


def finish_kernel(group, back, key, value, key_grad, value_grad, query_grad, filter_grad, skip_grad):
    rows, chans = key.shape

    def turned(at):
        return back[:, at * group : (at + 1) * group, :].reshape(chans, rows).T

    product_grad = turned(0)
    key_grad[...] = product_grad * value[...]
    value_grad[...] = product_grad * key[...]
    filter_grad[...] = turned(1)
    query_grad[...] = turned(2)
    skip_grad[...] = turned(3)[:1]


def finish(back, key, value, group):
    whole = jax.ShapeDtypeStruct(key.shape, jnp.float32)
    return pl.pallas_call(
        lambda *refs: finish_kernel(group, *refs),
        out_shape=[whole] * 4 + [jax.ShapeDtypeStruct((1, key.shape[1]), jnp.float32)],
        in_specs=[VMEM] * 3,
        out_specs=[VMEM] * 5,
        compiler_params=params(),
        cost_estimate=cost(0, 1 << 20),
    )(back, key, value)


def across(block, target):
    pairs = []
    for h in range(2):
        for m in range(2):
            to_h, to_m = target(h, m)
            pairs.append((h * 2 + m, to_h * 2 + to_m))
    return lax.ppermute(block, ("h", "m"), pairs)


def other_core(block):
    return lax.ppermute(block, "k", [(0, 1), (1, 0)])


def fold(pair, at, axis, apart):
    pairs = [(here, here ^ apart) for here in range(lax.axis_size(axis))]
    return pick(pair, at) + lax.ppermute(pick(pair, 1 - at), axis, pairs)


def pick(pair, at):
    return lax.dynamic_index_in_dim(pair, at, 0, False)


def local(key_branch, value_branch, query_branch, long_filter, skip_weight, out_weight, cotangent):
    rows, chans = key_branch.shape
    n_ctx = 32
    group = chans // n_ctx
    seq_len = rows * n_ctx
    norm_scale = 1.0 / math.sqrt(seq_len)
    tab = tables(seq_len)
    at_m, at_k = (lax.axis_index(name).astype(jnp.int32).reshape(1) for name in ("m", "k"))
    at_x = lax.axis_index("x")
    at_ctx = lax.axis_index(CTX)

    weights = lax.all_gather(out_weight, PLANE, axis=1, tiled=True)

    cot_same = across(cotangent, lambda h, m: (m, h))
    cot_swap = across(cotangent, lambda h, m: (m, 1 - h))

    sent = prepare(key_branch, value_branch, long_filter, query_branch, (), norm_scale, n_ctx)
    signals = lax.all_to_all(sent, CTX, 0, 0)
    product, query = signals[:, :group], signals[:, 2 * group :]

    spectra = forward_fourier(signals[:, : 2 * group], tab)
    prod_real, prod_imag = halves(spectra[:, :group])
    taps_real, taps_imag = halves(spectra[:, group:])
    conv = inverse_fourier(
        prod_real * taps_real - prod_imag * taps_imag, prod_real * taps_imag + prod_imag * taps_real, tab
    )
    skip = jnp.broadcast_to(lax.dynamic_slice(skip_weight, (at_ctx * group,), (group,))[:, None], (group, rows))
    gate = conv + skip[None] * product
    mixed = lax.all_to_all(double(gate * query, ()), CTX, 0, 0)

    near = line_blocks(cot_same, cot_swap, at_m, 4, (mixed,))
    near = lax.all_to_all(near, "l", 0, 0)
    far = other_core(near)

    partial = partial_sums(mixed, weights, at_k, True)
    partial = jnp.concatenate([other_core(partial[at : at + 2]) for at in range(0, 4, 2)])
    partial = partial_sums(mixed, weights, at_k, False, partial, (near,))
    line_got = lax.all_to_all(partial, "l", 0, 0)
    partial = line_got.sum(0)
    projected = across(pick(partial, at_m[0]), lambda h, m: (m, h))
    projected = projected + across(pick(partial, 1 - at_m[0]), lambda h, m: (1 - m, h))

    weight_part = outer(mixed, near, far, at_k)
    weight_part = lax.psum_scatter(weight_part, "y", scatter_dimension=0, tiled=True)
    weight_grad = fold(weight_part.reshape((2, 2) + weight_part.shape[1:]), at_x // 2, "x", 2)
    weight_grad = fold(weight_grad, at_x % 2, "x", 1) * norm_scale

    mixed_grad = gradient(weights, near, far, at_k, n_ctx)
    grad_got = lax.all_to_all(after(mixed_grad, (line_got,)), CTX, 0, 0)
    grad = grad_got.reshape(2, 16, 2, group, rows).sum(0).transpose(1, 0, 2, 3).reshape(n_ctx, group, rows)
    pre_grad = grad * query

    grad_real, grad_imag = halves(forward_fourier(pre_grad, tab))
    lead_real = jnp.concatenate([taps_real, prod_real], 1)
    lead_imag = jnp.concatenate([taps_imag, prod_imag], 1)
    grad_real = jnp.concatenate([grad_real, grad_real], 1)
    grad_imag = jnp.concatenate([grad_imag, grad_imag], 1)
    lagged = inverse_fourier(
        grad_real * lead_real + grad_imag * lead_imag, grad_imag * lead_real - grad_real * lead_imag, tab
    )
    back = returned(lagged, pre_grad, signals, grad, gate, skip, (projected, weight_part), norm_scale)
    back = lax.all_to_all(back, CTX, 0, 0)
    key_grad, value_grad, query_grad, filter_grad, skip_grad = finish(back, key_branch, value_branch, group)
    return (projected, key_grad, value_grad, query_grad, filter_grad, skip_grad.reshape(chans), weight_grad)


def solution(mesh):
    grid = Mesh(mesh.devices.reshape(SIZES), AXES)
    wide = P(("h", "y", "x"), ("m", "l", "k"))
    tall = P(("m", "l", "k"), ("h", "y", "x"))
    flat = P(("m", "l", "k"))
    return jax.shard_map(
        local,
        mesh=grid,
        in_specs=(wide, wide, wide, wide, flat, tall, wide),
        out_specs=(wide, wide, wide, wide, wide, flat, tall),
        check_vma=False,
    )
```
